512 devices in a mesh: leaf: 32 (over z_hi, y), expert: 8 (over x, core), mp: 2 (over z_lo).
Axes of the slice: x: 4, y: 8, z: 8 (z_hi: 4, z_lo: 2; z = z_hi * 2 + z_lo), core: 2. Of those that a mesh axis runs over, the one named last changes fastest.
Arguments:
- node_cache: bfloat16 [32, 8, 2, 256, 128], P('leaf', 'expert'), may hold values from -30 to 30
- node_hidden: bfloat16 [32, 6144], P('leaf', ('expert', 'mp')), may hold values from -6 to 6
- node_slot: int32 [32], replicated, may hold values from 0 to 31, each once
- parent: int32 [64], replicated, may hold values from 0 to 31, as said below
- child_query: bfloat16 [64, 4, 48, 128], P('leaf', None, ('expert', 'mp')), may hold values from -40 to 40
- child_kv: bfloat16 [64, 8, 2, 4, 128], P('leaf', 'expert'), may hold values from -6 to 6
- routes: int32 [64, 4, 2], P('leaf'), may hold values from 0 to 7, all different within a row; in each aligned block of 8 rows (0 to 7, 8 to 15, ..., all dimensions but the last counted through in order) at most 4 rows name the same one
- gate_w: float32 [64, 4, 2], P('leaf'), may hold values from 0.2 to 1
- w_gate: bfloat16 [8, 6144, 8192], P('expert', None, ('leaf', 'mp')), may hold values from -0.078125 to 0.078125
- w_up: bfloat16 [8, 6144, 8192], P('expert', None, ('leaf', 'mp')), may hold values from -0.078125 to 0.078125
- w_down: bfloat16 [8, 8192, 6144], P('expert', ('leaf', 'mp')), may hold values from -0.0625 to 0.0625
Outputs:
- mixed: bfloat16 [64, 4, 6144], P('leaf', None, ('expert', 'mp'))
The draws below stay inside these ranges and needn't reach their ends.
Inputs may be any that keep to these rules, and one draw needn't show every extreme that they name: `parent`: exactly 4 distinct node ids occur. `routes`: the two experts of a token differ; among the 8 tokens of one leaf index no expert is named more than 4 times.
All inputs are finite; a program needn't handle non-finite values.
Results may differ from the reference program's by a relative error of at most 0.013.
Values may be sent and summed in bfloat16 or wider, within the bound.
A program may use at most 64 MiB of HBM per device.

```python
import math
import jax
import jax.numpy as jnp
import numpy as np
from jax import lax

D = 6144
HQ = 48
KVH = 8
HD = 128
EXPERTS = 8
FFW = 8192
LBLK = 256
CHILD_DEV = 2
STEPS = 4
FORKS = 4
NODES = 32
CHILDREN = 64
CAP = 4
N_LEAF = 32


def draw_node_cache(key, part):
    key = jax.random.fold_in(key, 11)
    values = jnp.clip(jax.random.normal(key, (NODES, KVH, 2, LBLK, HD), jnp.float32), -6.0, 6.0)
    return values.astype(jnp.bfloat16)


def draw_child_query(key, part):
    key = jax.random.fold_in(key, 12)
    key_one = jax.random.fold_in(key, 0)
    values = jnp.clip(jax.random.normal(key_one, (CHILDREN, STEPS, HQ, HD), jnp.float32), -6.0, 6.0)
    return values.astype(jnp.bfloat16)


def draw_parent(key, part):
    key = jax.random.fold_in(key, 13)
    key_one, key_two, key_three = jax.random.split(key, 3)
    inner = (jax.random.permutation(key_one, NODES - 2)[:FORKS - 2] + 1).astype(jnp.int32)
    ends = jnp.array([0, NODES - 1], jnp.int32)
    chosen = jnp.concatenate([ends, inner])
    chosen = chosen[jax.random.permutation(key_three, FORKS)]
    fork_of = jax.random.randint(key_two, (CHILDREN,), 0, FORKS)
    fork_of = fork_of.at[:FORKS].set(jnp.arange(FORKS))
    return chosen[fork_of].astype(jnp.int32)


def steps_of(own_key, extent, shards, smallest, largest):
    loudness = 1.0
    for axis_at, blocks in shards:
        heights = jax.random.uniform(jax.random.fold_in(jax.random.fold_in(own_key, 6), axis_at), (blocks,), jnp.float32, smallest / len(shards), largest / len(shards))
        loudness = loudness * jnp.repeat(jnp.exp(heights), extent[axis_at] // blocks).reshape((-1,) + (1,) * (len(extent) - 1 - axis_at))
    return loudness


def routed_block(rng, own, number, rows, amount, top, most, skew):
    sequence = jax.random.permutation(rng, amount)
    heavy_load, usual = shares(amount, rows * top, most, skew, True), shares(amount, rows * top, most, skew, False)
    places = jnp.arange(amount)

    def named(lengths, turn):
        used = int((lengths > 0).sum())
        fixed = max(1, used // 4)
        moved = fixed + (places - fixed + turn * (used - fixed)) % max(1, amount - fixed)
        return jnp.zeros((amount,), jnp.int32).at[sequence[jnp.where(places < fixed, places, moved)]].set(jnp.asarray(lengths, jnp.int32))

    lengths = jnp.where(number % 4 == 0, named(heavy_load, number // 4), named(usual, number - number // 4 - 1))
    mixed = jax.random.permutation(jax.random.fold_in(own, 3), amount)
    giver, sink = mixed[0:amount // 2 * 2:2], mixed[1:amount // 2 * 2:2]
    margin = jnp.minimum(lengths[giver] - 1, most - lengths[sink]) // 2
    margin = jnp.where((giver == sequence[0]) | (sink == sequence[0]) | (lengths[sink] == 0), 0, jnp.maximum(margin, 0))
    moved = jax.random.randint(jax.random.fold_in(own, 4), (amount // 2,), 0, 1 << 20) % (margin + 1)
    lengths = lengths.at[giver].add(-moved).at[sink].add(moved)
    items = jnp.searchsorted(jnp.cumsum(lengths), jnp.arange(rows * top), side="right").astype(jnp.int32)
    listing = items.reshape(top, rows).T
    listing = listing[jax.random.permutation(jax.random.fold_in(own, 1), rows)]
    turn = jax.random.randint(jax.random.fold_in(own, 2), (rows, 1), 0, top)
    return jnp.take_along_axis(listing, (jnp.arange(top)[None, :] + turn) % top, axis=1)


def shares(count, total, most, skew, full):
    portions = [(1 << 20) // math.isqrt(standing ** skew) + 1 for standing in range(1, count + 1)]
    largest = most if full else min(most, max(-(-total // count), total * portions[0] // sum(portions)))
    least = 1 if total - largest >= count - 1 else 0
    holding, surplus = [largest] + [least] * (count - 1), total - largest - least * (count - 1)
    while surplus > 0:
        candidates = [i for i in range(1, count) if holding[i] < largest] or [i for i in range(1, count) if holding[i] < most]
        pool, left = sum([portions[i] for i in candidates]), surplus
        for i in candidates:
            extra = min(most - holding[i], max(1, left * portions[i] // pool), surplus)
            holding[i] = holding[i] + extra
            surplus = surplus - extra
    return np.array(holding)


def scatter_about(own_key, extent, spread, most, cuts=(), held_as=jnp.bfloat16):
    factor_of = steps_of(own_key, extent, cuts, -0.22, 0.18) if cuts else 1.0
    entries = jax.random.normal(own_key, extent, jnp.float32) * spread * factor_of
    return jnp.minimum(jnp.maximum(entries, -most), most).astype(held_as)


def setup_inputs(seed: int = 0) -> dict:
    keys = jax.random.split(jax.random.key(seed), 12)
    node_cache = draw_node_cache(jax.random.fold_in(keys[11], 71), 0)
    node_hidden = scatter_about(keys[1], (NODES, D), 1.0, 6.0, ((0, 32), (1, 16)))
    node_slot = jax.random.permutation(keys[2], NODES).astype(jnp.int32)
    parent = draw_parent(jax.random.fold_in(keys[11], 71), 0)
    child_query = draw_child_query(jax.random.fold_in(keys[11], 71), 0)
    child_kv = scatter_about(keys[5], (CHILDREN, KVH, 2, STEPS, HD), 1.0, 6.0, ((0, 32), (1, 8)))
    routes_keys = jax.random.split(jax.random.fold_in(keys[6], 1), CHILDREN * STEPS // (CHILD_DEV * STEPS))
    routes_turns = jax.random.permutation(jax.random.fold_in(keys[6], 3), CHILDREN * STEPS // (CHILD_DEV * STEPS))
    routes = jax.vmap(lambda own, number: routed_block(jax.random.fold_in(keys[6], 2), own, number, CHILD_DEV * STEPS, EXPERTS, 2, CAP, 2))(routes_keys, routes_turns).reshape((CHILDREN, STEPS, 2))
    gate_w = jnp.clip(0.2 + 0.8 * jax.random.uniform(keys[7], (CHILDREN, STEPS, 2), jnp.float32) ** steps_of(keys[7], (CHILDREN, STEPS, 2), ((0, 32),), -0.2, 0.2), 0.2, 1.0)
    w_gate = scatter_about(keys[8], (EXPERTS, D, FFW), D ** -0.5, 0.078125, ((0, 8), (2, 64)))
    w_up = scatter_about(keys[9], (EXPERTS, D, FFW), D ** -0.5, 0.078125, ((0, 8), (2, 64)))
    w_down = scatter_about(keys[10], (EXPERTS, FFW, D), FFW ** -0.5, 0.0625, ((0, 8), (1, 64)))
    return dict(node_cache=node_cache, node_hidden=node_hidden, node_slot=node_slot, parent=parent, child_query=child_query, child_kv=child_kv, routes=routes, gate_w=gate_w, w_gate=w_gate, w_up=w_up, w_down=w_down)


def reference(node_cache, node_hidden, node_slot, parent, child_query, child_kv, routes, gate_w, w_gate, w_up, w_down):
    group = HQ // KVH
    scale = 1.0 / (HD ** 0.5)
    parent_rows = node_slot[parent]
    parent_cache = node_cache[parent_rows]
    parent_row = node_hidden[parent_rows]
    queries = child_query.astype(jnp.float32).reshape(CHILDREN, STEPS, KVH, group, HD)
    key_rows = jnp.concatenate([parent_cache[:, :, 0], child_kv[:, :, 0]], axis=2).astype(jnp.float32)
    value_rows = jnp.concatenate([parent_cache[:, :, 1], child_kv[:, :, 1]], axis=2).astype(jnp.float32)
    scores = jnp.einsum('cskgd,ckpd->cskgp', queries, key_rows) * scale
    positions = jnp.arange(LBLK + STEPS)
    allowed = positions[None, :] < (LBLK + 1 + jnp.arange(STEPS))[:, None]
    scores = jnp.where(allowed[None, :, None, None, :], scores, -1e30)
    row_max = jnp.max(scores, axis=-1, keepdims=True)
    expon = jnp.exp(scores - row_max)
    weights = expon / jnp.sum(expon, axis=-1, keepdims=True)
    probs_bf = lax.optimization_barrier(weights.astype(jnp.bfloat16)).astype(jnp.float32)
    attn = jnp.einsum('cskgp,ckpd->cskgd', probs_bf, value_rows).reshape(CHILDREN, STEPS, D)
    hidden_x = (parent_row.astype(jnp.float32)[:, None, :] + attn).astype(jnp.bfloat16)
    row_total = CHILDREN * STEPS
    block_rows = CHILD_DEV * STEPS
    x_rows = hidden_x.reshape(row_total, D)
    flat_routes = routes.reshape(N_LEAF, 2 * block_rows)
    order = jnp.arange(2 * block_rows)
    earlier = (flat_routes[:, :, None] == flat_routes[:, None, :]) & (order[None, None, :] < order[None, :, None])
    slot_rank = jnp.sum(earlier.astype(jnp.int32), axis=2)
    slot_index = (jnp.arange(N_LEAF, dtype=jnp.int32)[:, None] * CAP + slot_rank).reshape(-1)
    expert_of = routes.reshape(-1)
    gate_values = gate_w.reshape(-1).astype(jnp.float32)
    x_assign = jnp.repeat(x_rows, 2, axis=0)
    slot_ids = jnp.arange(N_LEAF * CAP, dtype=jnp.int32)

    def one_expert(running, members):
        gate_mat, up_mat, down_mat, expert_id = members
        chosen = (slot_index[None, :] == slot_ids[:, None]) & (expert_of[None, :] == expert_id)
        packed = jnp.dot(chosen.astype(jnp.bfloat16), x_assign, preferred_element_type=jnp.float32).astype(jnp.bfloat16)
        gate_part = jnp.dot(packed, gate_mat, preferred_element_type=jnp.float32)
        up_part = jnp.dot(packed, up_mat, preferred_element_type=jnp.float32)
        hid_units = (jax.nn.silu(gate_part) * up_part).astype(jnp.bfloat16)
        expert_out = jnp.dot(hid_units, down_mat, preferred_element_type=jnp.float32).astype(jnp.bfloat16)
        weight_mat = chosen.astype(jnp.float32) * gate_values[None, :]
        delta = jnp.dot(weight_mat.T, expert_out.astype(jnp.float32), precision=lax.Precision.HIGHEST)
        return running + delta, None

    start_sum = jnp.zeros((2 * row_total, D), jnp.float32)
    summed, _ = lax.scan(one_expert, start_sum, (w_gate, w_up, w_down, jnp.arange(EXPERTS, dtype=jnp.int32)))
    delta_rows = summed.reshape(row_total, 2, D).sum(axis=1)
    mixed = (x_rows.astype(jnp.float32) + delta_rows).astype(jnp.bfloat16)
    return mixed.reshape(CHILDREN, STEPS, D)
```

```python
import functools

import jax
import jax.numpy as jnp
from jax import lax
from jax.experimental import pallas as pl
from jax.experimental.pallas import tpu as pltpu
from jax.sharding import PartitionSpec as P

F32 = jnp.float32
BF = jnp.bfloat16
SEMS = 256
LANES = 128
TOK = 8
HEADS = 3
NY = 8


class Ring:
    def __init__(self, size, me, device):
        self.size = size
        self.me = me
        self.device = device

    def at(self, offset):
        return lax.rem(self.me + offset + 2 * self.size, self.size)

    def right(self):
        return self.device(self.at(1))

    def left(self):
        return self.device(self.at(-1))


def interleave(jobs):
    jobs = list(jobs)
    while jobs:
        alive = []
        for job in jobs:
            try:
                next(job)
                alive.append(job)
            except StopIteration:
                pass
        jobs = alive


def kernel(
    geom,
    a_ref,
    b_ref,
    sel_ref,
    hid_ref,
    cache_ref,
    wg_ref,
    wu_ref,
    wd_ref,
    out_ref,
    scr,
):
    nx, ny, zh_n, zl_n = geom
    nz = zh_n * zl_n
    leaves = zh_n * ny
    tokens = leaves * TOK
    width = HEADS * LANES

    leaf = lax.axis_index("leaf")
    expert = lax.axis_index("expert")
    mp = lax.axis_index("mp")
    y = lax.rem(leaf, ny)
    zh = lax.div(leaf, ny)
    x = lax.div(expert, 2)
    core = lax.rem(expert, 2)
    z = zh * zl_n + mp

    def dev_x(k):
        return {"leaf": leaf, "expert": k * 2 + core, "mp": mp}

    def dev_y(k):
        return {"leaf": zh * ny + k, "expert": expert, "mp": mp}

    def dev_zh(k):
        return {"leaf": k * ny + y, "expert": expert, "mp": mp}

    def dev_z(k):
        return {
            "leaf": lax.div(k, zl_n) * ny + y,
            "expert": expert,
            "mp": lax.rem(k, zl_n),
        }

    sibling = {"leaf": leaf, "expert": x * 2 + (1 - core), "mp": mp}
    rx = Ring(nx, x, dev_x)
    ry = Ring(ny, y, dev_y)
    rz = Ring(nz, z, dev_z)
    rzh = Ring(zh_n, zh, dev_zh)

    send_sems, recv_sems, load_sems = scr["send"], scr["recv"], scr["load"]
    count = [0]
    sent = []

    def copy(src, dst, device):
        i = count[0]
        count[0] += 1
        c = pltpu.make_async_remote_copy(
            src_ref=src,
            dst_ref=dst,
            send_sem=send_sems.at[i],
            recv_sem=recv_sems.at[i],
            device_id=device,
            device_id_type=pl.DeviceIdType.MESH,
        )
        c.start()
        sent.append(c)
        return i

    def arrive(dst, i):
        pltpu.make_async_remote_copy(
            src_ref=dst,
            dst_ref=dst,
            send_sem=send_sems.at[i],
            recv_sem=recv_sems.at[i],
            device_id=sibling,
            device_id_type=pl.DeviceIdType.MESH,
        ).wait_recv()

    def gather(buf, ring, split, got=None):
        half = ring.size // 2
        right, left = ring.right(), ring.left()
        for s in range(1, half + 1):
            sp, sm = ring.at(1 - s), ring.at(s - 1)
            gp, gm = ring.at(-s), ring.at(s)
            if s < half:
                src_p, src_m = buf.at[sp], buf.at[sm]
                got_p, got_m = buf.at[gp], buf.at[gm]
            elif split:
                n = buf.shape[1] // 2
                src_p, src_m = buf.at[sp, pl.ds(0, n)], buf.at[sm, pl.ds(n, n)]
                got_p, got_m = buf.at[gp, pl.ds(0, n)], buf.at[gm, pl.ds(n, n)]
            else:
                src_p, src_m = buf.at[sp], None
                got_p, got_m = buf.at[gp], None
            ip = copy(src_p, src_p, right)
            if src_m is not None:
                im = copy(src_m, src_m, left)
            yield
            arrive(got_p, ip)
            if s == half and split:
                if got is not None:
                    n = buf.shape[1] // 2
                    got((gp, pl.ds(0, n)))
                arrive(got_m, im)
                if got is not None:
                    got((gm, pl.ds(n, n)))
            else:
                if got is not None:
                    got((gp,))
                if got_m is not None:
                    arrive(got_m, im)
                    if got is not None:
                        got((gm,))

    def add_into(ref, index, other, oindex):
        ref[index] = (ref[index].astype(F32) + other[oindex].astype(F32)).astype(BF)

    def scatter(h, rp, rm, ring, split, finish):
        half = ring.size // 2
        right, left = ring.right(), ring.left()
        n = h.shape[1] // 2
        lo, hi = pl.ds(0, n), pl.ds(n, n)
        for s in range(1, half + 1):
            dp, dm = ring.at(half - s + 1), ring.at(s - half - 1)
            if s == 1:
                if split:
                    ip = copy(h.at[dp, lo], rp.at[0, lo], right)
                    im = copy(h.at[dm, hi], rm.at[0, hi], left)
                else:
                    ip = copy(h.at[dp], rp.at[0], right)
                    im = None
            else:
                if s == 2:
                    if split:
                        add_into(rp, (0, lo), h, (dp, lo))
                        rp[0, hi] = h[dp, hi]
                        add_into(rm, (0, hi), h, (dm, hi))
                        rm[0, lo] = h[dm, lo]
                    else:
                        add_into(rp, 0, h, dp)
                else:
                    add_into(rp, s - 2, h, dp)
                    add_into(rm, s - 2, h, dm)
                ip = copy(rp.at[s - 2], rp.at[s - 1], right)
                if s == 2 and not split:
                    im = copy(h.at[dm], rm.at[1], left)
                else:
                    im = copy(rm.at[s - 2], rm.at[s - 1], left)
            yield
            if s == 1 and split:
                arrive(rp.at[0, lo], ip)
                arrive(rm.at[0, hi], im)
            else:
                arrive(rp.at[s - 1], ip)
                if im is not None:
                    arrive(rm.at[s - 1], im)
        me = ring.me
        if half > 1:
            finish(
                h[me].astype(F32)
                + rp[half - 1].astype(F32)
                + rm[half - 1].astype(F32)
            )
        elif split:
            first = h[me, lo].astype(F32) + rp[0, lo].astype(F32)
            second = h[me, hi].astype(F32) + rm[0, hi].astype(F32)
            finish(jnp.concatenate([first, second], axis=0))
        else:
            finish(h[me].astype(F32) + rp[0].astype(F32))

    loads = [
        pltpu.make_async_copy(wg_ref.at[0], scr["wgu"].at[:, pl.ds(0, LANES)], load_sems.at[0]),
        pltpu.make_async_copy(wu_ref.at[0], scr["wgu"].at[:, pl.ds(LANES, LANES)], load_sems.at[1]),
        pltpu.make_async_copy(wd_ref.at[0], scr["wd"], load_sems.at[2]),
    ]
    for c in loads:
        c.start()

    abuf, bbuf = scr["abuf"], scr["bbuf"]
    abuf[y, zh] = a_ref[...]
    bbuf[zh, y] = b_ref[...]

    barrier = pltpu.get_barrier_semaphore()
    partners = [sibling]
    for ring in (rx, ry, rz, rzh):
        partners += [ring.right(), ring.left()]
    for partner in partners:
        pl.semaphore_signal(barrier, inc=1, device_id=partner, device_id_type=pl.DeviceIdType.MESH)
    pl.semaphore_wait(barrier, len(partners))

    def gather_a():
        yield from gather(abuf.at[y], rzh, False)
        yield from gather(abuf, ry, True)

    def gather_b():
        yield from gather(bbuf.at[zh], ry, False)
        yield from gather(bbuf, rzh, True)

    interleave([gather_a(), gather_b()])

    def rows_a(k):
        return jnp.concatenate(
            [
                abuf[:, i, pl.ds(k * TOK, TOK)].astype(F32).reshape(ny * TOK, LANES)
                for i in range(zh_n)
            ],
            axis=0,
        )

    new_k = bbuf[:, :, pl.ds(0, TOK)].astype(F32).reshape(tokens, LANES).astype(BF)
    new_v = bbuf[:, :, pl.ds(TOK, TOK)].astype(F32).reshape(tokens, LANES).astype(BF)
    old_k = cache_ref[0]
    old_v = cache_ref[1]
    contract = (((1,), (1,)), ((), ()))
    row_id = lax.broadcasted_iota(jnp.int32, (tokens, tokens), 0)
    col_id = lax.broadcasted_iota(jnp.int32, (tokens, tokens), 1)
    allowed = (row_id // 4 == col_id // 4) & (col_id <= row_id)
    scale = 1.0 / LANES**0.5
    mine = sel_ref[...]
    xp = [scr["xp0"], scr["xp1"], scr["xp2"]]
    for p in range(HEADS):
        q = rows_a(p).astype(BF)
        s_old = lax.dot_general(q, old_k, contract, preferred_element_type=F32) * scale
        s_new = lax.dot_general(q, new_k, contract, preferred_element_type=F32) * scale
        s_new = jnp.where(allowed, s_new, -1e30)
        top = jnp.maximum(
            jnp.max(s_old, axis=1, keepdims=True), jnp.max(s_new, axis=1, keepdims=True)
        )
        e_old = jnp.exp(s_old - top)
        e_new = jnp.exp(s_new - top)
        total = jnp.sum(e_old, axis=1, keepdims=True) + jnp.sum(e_new, axis=1, keepdims=True)
        inv = 1.0 / total
        attn = jnp.dot((e_old * inv).astype(BF), old_v, preferred_element_type=F32)
        attn += jnp.dot((e_new * inv).astype(BF), new_v, preferred_element_type=F32)
        row = hid_ref[:, pl.ds(p * LANES, LANES)].astype(F32)
        here = jnp.where(mine > 0.5, attn + row, 0.0)
        here = here.reshape(zh_n, ny, TOK, LANES)
        if p < 2:
            for i in range(zh_n):
                xp[p][:, i] = here[i].astype(BF)
        else:
            xp[p][...] = here.astype(BF)

    own = [scr["own0"], scr["own1"], scr["own2"]]
    rp = scr["xrp"]
    rm = scr["xrm"]
    mids = scr["xmid"]
    xs = scr["xs"]

    def own_at(p):
        if p == 0:
            return own[0].at[z, y]
        if p == 1:
            return own[1].at[x, z]
        return own[2].at[y, x]

    def home(p):
        first, second = (ry, rzh) if p < 2 else (rzh, ry)

        def keep(v):
            mids[p][...] = v.astype(BF)

        yield from scatter(xp[p], rp[p][0], rm[p][0], first, True, keep)

        def final(v):
            w = v.astype(BF)
            xs[p] = w
            if p == 0:
                own[0][z, y, x] = w
            elif p == 1:
                own[1][x, z, y] = w
            else:
                own[2][y, x, z] = w

        yield from scatter(mids[p], rp[p][1], rm[p][1], second, False, final)

    interleave([home(p) for p in range(HEADS)])

    sib = [scr["sib0"], scr["sib1"], scr["sib2"]]
    d2d = []
    orders = [(rx, ry, rz), (ry, rz, rx), (rz, rx, ry)]

    def everywhere(p):
        one, two, three = orders[p]
        yield from gather(own_at(p), one, False)
        last = own[p].at[three.me]
        yield from gather(last, two, True)

        def forward(index):
            i = copy(own[p].at[index], sib[p].at[index], sibling)
            d2d.append((sib[p].at[index], i))

        forward((three.me,))
        yield from gather(own[p], three, True, forward)

    interleave([everywhere(p) for p in range(HEADS)])

    def tiles(refs, p, xi, m, i):
        zi = i * zl_n + m
        if p == 0:
            return refs[0].at[zi, :, xi]
        if p == 1:
            return refs[1].at[xi, zi]
        return refs[2].at[:, xi, zi]

    acc = scr["acc"]
    acc[...] = jnp.zeros_like(acc)
    for c in loads:
        c.wait()
    blocks = nx * zl_n

    def up(refs, which):
        @pl.loop(0, blocks)
        def _(j):
            xi, m = lax.div(j, zl_n), lax.rem(j, zl_n)
            cols = []
            for p in range(HEADS):
                cols.append(
                    jnp.concatenate(
                        [
                            tiles(refs, p, xi, m, i)[...].astype(F32).reshape(ny * TOK, LANES)
                            for i in range(zh_n)
                        ],
                        axis=0,
                    ).astype(BF)
                )
            rows = jnp.concatenate(cols, axis=1)
            off = pl.multiple_of(((xi * 2 + which) * zl_n + m) * width, LANES)
            acc[...] += jnp.dot(rows, scr["wgu"][pl.ds(off, width), :], preferred_element_type=F32)

    up(own, core)
    for ref, i in d2d:
        arrive(ref, i)
    up(sib, 1 - core)

    gates = rows_a(HEADS)
    gate = gates[:, 0:1] + gates[:, 1:2]
    g = acc[:, pl.ds(0, LANES)]
    u = acc[:, pl.ds(LANES, LANES)]
    units = (g * (1.0 / (1.0 + jnp.exp(-g))) * u).astype(BF).astype(F32)
    scr["units"][...] = (units * gate).astype(BF)

    hs = [scr["hs0"], scr["hs1"], scr["hs2"]]
    ho = [scr["ho0"], scr["ho1"], scr["ho2"]]
    hr = [scr["hr0"], scr["hr1"], scr["hr2"]]

    def down(refs, which):
        @pl.loop(0, blocks)
        def _(j):
            xi, m = lax.div(j, zl_n), lax.rem(j, zl_n)
            off = pl.multiple_of(((xi * 2 + which) * zl_n + m) * width, LANES)
            o = jnp.dot(
                scr["units"][...], scr["wd"][:, pl.ds(off, width)], preferred_element_type=F32
            )
            for p in range(HEADS):
                part = o[:, p * LANES : (p + 1) * LANES].reshape(zh_n, ny, TOK, LANES)
                for i in range(zh_n):
                    tiles(refs, p, xi, m, i)[...] = part[i].astype(BF)

    down(hs, 1 - core)
    crossing = [copy(hs[p], hr[p], sibling) for p in range(HEADS)]
    down(ho, core)
    for p in range(HEADS):
        arrive(hr[p], crossing[p])

        @pl.loop(0, ho[p].shape[0])
        def _(k):
            add_into(ho[p], k, hr[p], k)

    grp, grm = scr["grp"], scr["grm"]
    gmid = scr["gmid"]

    def back(p):
        one, two, three = orders[p]

        def keep(level):
            def write(v):
                gmid[p][level][...] = v.astype(BF)

            return write

        yield from scatter(ho[p], grp[p][0], grm[p][0], three, True, keep(0))
        yield from scatter(gmid[p][0], grp[p][1], grm[p][1], two, True, keep(1))

        def final(v):
            out_ref[:, pl.ds(p * LANES, LANES)] = (xs[p].astype(F32) + v).astype(BF)

        yield from scatter(gmid[p][1], grp[p][2], grm[p][2], one, False, final)

    interleave([back(p) for p in range(HEADS)])

    for c in sent:
        c.wait_send()


def scratch_of(geom, features):
    nx, ny, zh_n, zl_n = geom
    nz = zh_n * zl_n
    tokens = zh_n * ny * TOK
    tile = (TOK, LANES)
    vm = lambda *shape: pltpu.VMEM(shape + tile, BF)
    full = [(nz, ny, nx), (nx, nz, ny), (ny, nx, nz)]
    scr = {
        "send": pltpu.SemaphoreType.DMA((SEMS,)),
        "recv": pltpu.SemaphoreType.DMA((SEMS,)),
        "load": pltpu.SemaphoreType.DMA((3,)),
        "wgu": pltpu.VMEM((features, 2 * LANES), BF),
        "wd": pltpu.VMEM((LANES, features), BF),
        "abuf": pltpu.VMEM((ny, zh_n, 32, LANES), BF),
        "bbuf": pltpu.VMEM((zh_n, ny, 16, LANES), BF),
        "xs": vm(HEADS),
        "acc": pltpu.VMEM((tokens, 2 * LANES), F32),
        "units": pltpu.VMEM((tokens, LANES), BF),
    }
    for p in range(HEADS):
        a, b, c = full[p]
        for name in ("own", "sib", "hs", "ho", "hr"):
            scr[name + str(p)] = vm(a, b, c)
        scr["xp" + str(p)] = vm(ny, zh_n) if p < 2 else vm(zh_n, ny)
    scr["xmid"] = [vm(zh_n), vm(zh_n), vm(ny)]
    halves = lambda n: max(n // 2, 1)
    scr["xrp"] = []
    scr["xrm"] = []
    scr["grp"] = []
    scr["grm"] = []
    scr["gmid"] = []
    for p in range(HEADS):
        first, second = (ny, zh_n) if p < 2 else (zh_n, ny)
        a, b, c = full[p]
        for key in ("xrp", "xrm"):
            scr[key].append([vm(halves(first), second), vm(halves(second))])
        for key in ("grp", "grm"):
            scr[key].append([vm(halves(a), b, c), vm(halves(b), c), vm(halves(c))])
        scr["gmid"].append([vm(b, c), vm(c)])
    return scr


def local(
    geom,
    node_cache,
    node_hidden,
    node_slot,
    parent,
    child_query,
    child_kv,
    routes,
    gate_w,
    w_gate,
    w_up,
    w_down,
):
    nx, ny, zh_n, zl_n = geom
    leaf = lax.axis_index("leaf")
    expert = lax.axis_index("expert")
    queries = child_query.reshape(TOK, HEADS, LANES).transpose(1, 0, 2).reshape(HEADS * TOK, LANES)
    weight = jnp.sum(jnp.where(routes == expert, gate_w, 0.0), axis=-1).reshape(TOK, 1)
    high = weight.astype(BF).astype(F32)
    lane = jnp.arange(LANES)[None, :]
    gates = jnp.where(lane == 0, high, jnp.where(lane == 1, weight - high, 0.0)).astype(BF)
    a = jnp.concatenate([queries, gates], axis=0)
    b = child_kv[:, 0].transpose(1, 0, 2, 3).reshape(2 * TOK, LANES)
    node = jnp.sum(jnp.where(node_slot == leaf, jnp.arange(node_slot.shape[0]), 0))
    mine = jnp.broadcast_to((parent == node).astype(F32)[:, None], (parent.shape[0], 4))
    mine = jnp.broadcast_to(mine.reshape(-1, 1), (parent.shape[0] * 4, LANES))
    features = w_gate.shape[1]
    vmem = pl.BlockSpec(memory_space=pltpu.VMEM)
    hbm = pl.BlockSpec(memory_space=pl.ANY)
    out = pl.pallas_call(
        functools.partial(kernel, geom),
        out_shape=jax.ShapeDtypeStruct((TOK, HEADS * LANES), BF),
        in_specs=[vmem] * 5 + [hbm] * 3,
        out_specs=vmem,
        scratch_shapes=[scratch_of(geom, features)],
        compiler_params=pltpu.CompilerParams(
            collective_id=0, has_side_effects=True, vmem_limit_bytes=58 * 1024 * 1024
        ),
    )(a, b, mine, node_hidden, node_cache[0, 0], w_gate, w_up, w_down)
    return out.reshape(child_query.shape[0], child_query.shape[1], HEADS * LANES)


def solution(mesh):
    leaves, experts, mp = mesh.shape["leaf"], mesh.shape["expert"], mesh.shape["mp"]
    geom = (experts // 2, NY, leaves // NY, mp)
    in_specs = (
        P("leaf", "expert", None, None, None),
        P("leaf", ("expert", "mp")),
        P(),
        P(),
        P("leaf", None, ("expert", "mp"), None),
        P("leaf", "expert", None, None, None),
        P("leaf", None, None),
        P("leaf", None, None),
        P("expert", None, ("leaf", "mp")),
        P("expert", None, ("leaf", "mp")),
        P("expert", ("leaf", "mp"), None),
    )
    out_specs = P("leaf", None, ("expert", "mp"))
    return jax.shard_map(
        functools.partial(local, geom),
        mesh=mesh,
        in_specs=in_specs,
        out_specs=out_specs,
        check_vma=False,
    )
```

```python
import functools

import jax
import jax.numpy as jnp
from jax import lax
from jax.experimental import pallas as pl
from jax.experimental.pallas import tpu as pltpu
from jax.sharding import PartitionSpec as P

F32 = jnp.float32
BF = jnp.bfloat16
SEMS = 256
LANES = 128
TOK = 8
HEADS = 3
NY = 8


class Ring:
    def __init__(self, size, me, device):
        self.size = size
        self.me = me
        self.device = device

    def at(self, offset):
        return lax.rem(self.me + offset + 2 * self.size, self.size)

    def near_first(self):
        return sorted(range(1, self.size), key=lambda k: (min(k, self.size - k), k))

    def far_first(self):
        return self.near_first()[::-1]


def interleave(jobs):
    jobs = list(jobs)
    while jobs:
        alive = []
        for job in jobs:
            try:
                next(job)
                alive.append(job)
            except StopIteration:
                pass
        jobs = alive


def kernel(
    geom,
    slot_ref,
    routes_ref,
    gate_ref,
    parent_ref,
    query_ref,
    kv_ref,
    hid_ref,
    cache_ref,
    wg_ref,
    wu_ref,
    wd_ref,
    out_ref,
    scr,
):
    nx, ny, zh_n, zl_n = geom
    nz = zh_n * zl_n
    leaves = zh_n * ny
    tokens = leaves * TOK
    width = HEADS * LANES

    leaf = lax.axis_index("leaf")
    expert = lax.axis_index("expert")
    mp = lax.axis_index("mp")
    y = lax.rem(leaf, ny)
    zh = lax.div(leaf, ny)
    x = lax.div(expert, 2)
    core = lax.rem(expert, 2)
    z = zh * zl_n + mp

    def dev_x(k):
        return {"leaf": leaf, "expert": k * 2 + core, "mp": mp}

    def dev_y(k):
        return {"leaf": zh * ny + k, "expert": expert, "mp": mp}

    def dev_zh(k):
        return {"leaf": k * ny + y, "expert": expert, "mp": mp}

    def dev_z(k):
        return {
            "leaf": lax.div(k, zl_n) * ny + y,
            "expert": expert,
            "mp": lax.rem(k, zl_n),
        }

    sibling = {"leaf": leaf, "expert": x * 2 + (1 - core), "mp": mp}
    rx = Ring(nx, x, dev_x)
    ry = Ring(ny, y, dev_y)
    rz = Ring(nz, z, dev_z)
    rzh = Ring(zh_n, zh, dev_zh)

    send_sems, recv_sems, load_sems = scr["send"], scr["recv"], scr["load"]
    count = [0]
    sent = []

    def copy(src, dst, device):
        i = count[0]
        count[0] += 1
        c = pltpu.make_async_remote_copy(
            src_ref=src,
            dst_ref=dst,
            send_sem=send_sems.at[i],
            recv_sem=recv_sems.at[i],
            device_id=device,
            device_id_type=pl.DeviceIdType.MESH,
        )
        c.start()
        sent.append(c)
        return i

    def arrive(dst, i):
        pltpu.make_async_remote_copy(
            src_ref=dst,
            dst_ref=dst,
            send_sem=send_sems.at[i],
            recv_sem=recv_sems.at[i],
            device_id=sibling,
            device_id_type=pl.DeviceIdType.MESH,
        ).wait_recv()

    def gather(buf, ring, got=None):
        ids = {}
        for k in ring.far_first():
            ids[k] = copy(buf.at[ring.me], buf.at[ring.me], ring.device(ring.at(k)))
        yield
        for k in ring.near_first():
            index = ring.at(-k)
            arrive(buf.at[index], ids[k])
            if got is not None:
                got(index)

    def add_into(ref, index, other, oindex):
        ref[index] = (ref[index].astype(F32) + other[oindex].astype(F32)).astype(BF)

    def scatter(h, r, ring, finish):
        ids = {}
        for k in ring.far_first():
            ids[k] = copy(h.at[ring.at(k)], r.at[k - 1], ring.device(ring.at(k)))
        yield
        total = h[ring.me].astype(F32)
        for k in ring.near_first():
            arrive(r.at[k - 1], ids[k])
            total = total + r[k - 1].astype(F32)
        finish(total)

    loads = [
        pltpu.make_async_copy(wg_ref.at[0], scr["wgu"].at[:, pl.ds(0, LANES)], load_sems.at[0]),
        pltpu.make_async_copy(wu_ref.at[0], scr["wgu"].at[:, pl.ds(LANES, LANES)], load_sems.at[1]),
        pltpu.make_async_copy(wd_ref.at[0], scr["wd"], load_sems.at[2]),
        pltpu.make_async_copy(cache_ref.at[0, 0], scr["cache"], load_sems.at[3]),
    ]
    for c in loads:
        c.start()

    abuf, bbuf = scr["abuf"], scr["bbuf"]
    row = lax.broadcasted_iota(jnp.int32, (TOK, LANES), 0)
    lane = lax.broadcasted_iota(jnp.int32, (TOK, LANES), 1)
    weight = jnp.zeros((TOK, LANES), F32)
    for t in range(TOK):
        w = jnp.float32(0.0)
        for k in range(2):
            w += jnp.where(
                routes_ref[t // 4, k, t % 4] == expert, gate_ref[t // 4, k, t % 4], 0.0
            )
        weight = jnp.where(row == t, w, weight)
    high = weight.astype(BF).astype(F32)
    for h in range(HEADS):
        abuf[y, zh, pl.ds(h * TOK, TOK)] = (
            query_ref[:, h].astype(F32).reshape(TOK, LANES).astype(BF)
        )
    abuf[y, zh, pl.ds(HEADS * TOK, TOK)] = jnp.where(
        lane == 0, high, jnp.where(lane == 1, weight - high, 0.0)
    ).astype(BF)
    for k in range(2):
        part = kv_ref[:, 0, k].astype(F32).reshape(TOK, LANES)
        bbuf[zh, y, pl.ds(k * TOK, TOK)] = part.astype(BF)

    barrier = pltpu.get_barrier_semaphore()
    partners = [sibling]
    for ring in (rx, ry, rz):
        partners += [ring.device(ring.at(k)) for k in range(1, ring.size)]
    for partner in partners:
        pl.semaphore_signal(barrier, inc=1, device_id=partner, device_id_type=pl.DeviceIdType.MESH)
    pl.semaphore_wait(barrier, len(partners))

    def gather_a():
        yield from gather(abuf.at[y], rzh)
        yield from gather(abuf, ry)

    def gather_b():
        yield from gather(bbuf.at[zh], ry)
        yield from gather(bbuf, rzh)

    interleave([gather_a(), gather_b()])

    def rows_a(k):
        return jnp.concatenate(
            [
                abuf[:, i, pl.ds(k * TOK, TOK)].astype(F32).reshape(ny * TOK, LANES)
                for i in range(zh_n)
            ],
            axis=0,
        )

    new_k = bbuf[:, :, pl.ds(0, TOK)].astype(F32).reshape(tokens, LANES).astype(BF)
    new_v = bbuf[:, :, pl.ds(TOK, TOK)].astype(F32).reshape(tokens, LANES).astype(BF)
    loads[3].wait()
    old_k = scr["cache"][0]
    old_v = scr["cache"][1]
    contract = (((1,), (1,)), ((), ()))
    row_id = lax.broadcasted_iota(jnp.int32, (tokens, tokens), 0)
    col_id = lax.broadcasted_iota(jnp.int32, (tokens, tokens), 1)
    allowed = (row_id // 4 == col_id // 4) & (col_id <= row_id)
    scale = 1.0 / LANES**0.5
    node = jnp.int32(0)
    for k in range(leaves):
        node += jnp.where(slot_ref[k] == leaf, k, 0)
    children = leaves * 2
    token_child = lax.broadcasted_iota(jnp.int32, (tokens, children), 0) // 4
    child_id = lax.broadcasted_iota(jnp.int32, (tokens, children), 1)
    here_row = (token_child == child_id) & (parent_ref[...] == node)
    mine = jnp.sum(jnp.where(here_row, 1.0, 0.0), axis=1, keepdims=True)
    xp = [scr["xp0"], scr["xp1"], scr["xp2"]]
    for p in range(HEADS):
        q = rows_a(p).astype(BF)
        s_old = lax.dot_general(q, old_k, contract, preferred_element_type=F32) * scale
        s_new = lax.dot_general(q, new_k, contract, preferred_element_type=F32) * scale
        s_new = jnp.where(allowed, s_new, -1e30)
        top = jnp.maximum(
            jnp.max(s_old, axis=1, keepdims=True), jnp.max(s_new, axis=1, keepdims=True)
        )
        e_old = jnp.exp(s_old - top)
        e_new = jnp.exp(s_new - top)
        total = jnp.sum(e_old, axis=1, keepdims=True) + jnp.sum(e_new, axis=1, keepdims=True)
        inv = 1.0 / total
        attn = jnp.dot((e_old * inv).astype(BF), old_v, preferred_element_type=F32)
        attn += jnp.dot((e_new * inv).astype(BF), new_v, preferred_element_type=F32)
        row = hid_ref[:, pl.ds(p * LANES, LANES)].astype(F32)
        here = jnp.where(mine > 0.5, attn + row, 0.0)
        here = here.reshape(zh_n, ny, TOK, LANES)
        if p < 2:
            for i in range(zh_n):
                xp[p][:, i] = here[i].astype(BF)
        else:
            xp[p][...] = here.astype(BF)

    own = [scr["own0"], scr["own1"], scr["own2"]]
    xr = scr["xr"]
    mids = scr["xmid"]
    xs = scr["xs"]

    def own_at(p):
        if p == 0:
            return own[0].at[z, y]
        if p == 1:
            return own[1].at[x, z]
        return own[2].at[y, x]

    def home(p):
        first, second = (ry, rzh) if p < 2 else (rzh, ry)

        def keep(v):
            mids[p][...] = v.astype(BF)

        yield from scatter(xp[p], xr[p][0], first, keep)

        def final(v):
            w = v.astype(BF)
            xs[p] = w
            if p == 0:
                own[0][z, y, x] = w
            elif p == 1:
                own[1][x, z, y] = w
            else:
                own[2][y, x, z] = w

        yield from scatter(mids[p], xr[p][1], second, final)

    interleave([home(p) for p in range(HEADS)])

    sib = [scr["sib0"], scr["sib1"], scr["sib2"]]
    d2d = []
    orders = [(rx, ry, rz), (ry, rz, rx), (rz, rx, ry)]

    def everywhere(p):
        one, two, three = orders[p]
        yield from gather(own_at(p), one)
        last = own[p].at[three.me]
        yield from gather(last, two)

        def forward(index):
            i = copy(own[p].at[index], sib[p].at[index], sibling)
            d2d.append((sib[p].at[index], i))

        forward(three.me)
        yield from gather(own[p], three, forward)

    interleave([everywhere(p) for p in range(HEADS)])

    def tiles(refs, p, xi, m, i):
        zi = i * zl_n + m
        if p == 0:
            return refs[0].at[zi, :, xi]
        if p == 1:
            return refs[1].at[xi, zi]
        return refs[2].at[:, xi, zi]

    acc = scr["acc"]
    acc[...] = jnp.zeros_like(acc)
    for c in loads[:3]:
        c.wait()
    blocks = nx * zl_n

    def up(refs, which):
        @pl.loop(0, blocks)
        def _(j):
            xi, m = lax.div(j, zl_n), lax.rem(j, zl_n)
            cols = []
            for p in range(HEADS):
                cols.append(
                    jnp.concatenate(
                        [
                            tiles(refs, p, xi, m, i)[...].astype(F32).reshape(ny * TOK, LANES)
                            for i in range(zh_n)
                        ],
                        axis=0,
                    ).astype(BF)
                )
            rows = jnp.concatenate(cols, axis=1)
            off = pl.multiple_of(((xi * 2 + which) * zl_n + m) * width, LANES)
            acc[...] += jnp.dot(rows, scr["wgu"][pl.ds(off, width), :], preferred_element_type=F32)

    up(own, core)
    for ref, i in d2d:
        arrive(ref, i)
    up(sib, 1 - core)

    gates = rows_a(HEADS)
    gate = gates[:, 0:1] + gates[:, 1:2]
    g = acc[:, pl.ds(0, LANES)]
    u = acc[:, pl.ds(LANES, LANES)]
    units = (g * (1.0 / (1.0 + jnp.exp(-g))) * u).astype(BF).astype(F32)
    scr["units"][...] = (units * gate).astype(BF)

    hs = [scr["hs0"], scr["hs1"], scr["hs2"]]
    ho = [scr["ho0"], scr["ho1"], scr["ho2"]]
    hr = [scr["hr0"], scr["hr1"], scr["hr2"]]

    def down(refs, which):
        @pl.loop(0, blocks)
        def _(j):
            xi, m = lax.div(j, zl_n), lax.rem(j, zl_n)
            off = pl.multiple_of(((xi * 2 + which) * zl_n + m) * width, LANES)
            o = jnp.dot(
                scr["units"][...], scr["wd"][:, pl.ds(off, width)], preferred_element_type=F32
            )
            for p in range(HEADS):
                part = o[:, p * LANES : (p + 1) * LANES].reshape(zh_n, ny, TOK, LANES)
                for i in range(zh_n):
                    tiles(refs, p, xi, m, i)[...] = part[i].astype(BF)

    down(hs, 1 - core)
    crossing = [copy(hs[p], hr[p], sibling) for p in range(HEADS)]
    down(ho, core)
    for p in range(HEADS):
        arrive(hr[p], crossing[p])

        @pl.loop(0, ho[p].shape[0])
        def _(k):
            add_into(ho[p], k, hr[p], k)

    gr = scr["gr"]
    gmid = scr["gmid"]

    def back(p):
        one, two, three = orders[p]

        def keep(level):
            def write(v):
                gmid[p][level][...] = v.astype(BF)

            return write

        yield from scatter(ho[p], gr[p][0], three, keep(0))
        yield from scatter(gmid[p][0], gr[p][1], two, keep(1))

        def final(v):
            w = (xs[p].astype(F32) + v).astype(BF)
            for c in range(2):
                out_ref[c, :, pl.ds(p * LANES, LANES)] = w[c * 4 : c * 4 + 4]

        yield from scatter(gmid[p][1], gr[p][2], one, final)

    interleave([back(p) for p in range(HEADS)])

    for c in sent:
        c.wait_send()


def scratch_of(geom, features):
    nx, ny, zh_n, zl_n = geom
    nz = zh_n * zl_n
    tokens = zh_n * ny * TOK
    tile = (TOK, LANES)
    vm = lambda *shape: pltpu.VMEM(shape + tile, BF)
    full = [(nz, ny, nx), (nx, nz, ny), (ny, nx, nz)]
    scr = {
        "send": pltpu.SemaphoreType.DMA((SEMS,)),
        "recv": pltpu.SemaphoreType.DMA((SEMS,)),
        "load": pltpu.SemaphoreType.DMA((4,)),
        "cache": pltpu.VMEM((2, 256, LANES), BF),
        "wgu": pltpu.VMEM((features, 2 * LANES), BF),
        "wd": pltpu.VMEM((LANES, features), BF),
        "abuf": pltpu.VMEM((ny, zh_n, 32, LANES), BF),
        "bbuf": pltpu.VMEM((zh_n, ny, 16, LANES), BF),
        "xs": vm(HEADS),
        "acc": pltpu.VMEM((tokens, 2 * LANES), F32),
        "units": pltpu.VMEM((tokens, LANES), BF),
    }
    for p in range(HEADS):
        a, b, c = full[p]
        for name in ("own", "sib", "hs", "ho", "hr"):
            scr[name + str(p)] = vm(a, b, c)
        scr["xp" + str(p)] = vm(ny, zh_n) if p < 2 else vm(zh_n, ny)
    scr["xmid"] = [vm(zh_n), vm(zh_n), vm(ny)]
    scr["xr"] = []
    scr["gr"] = []
    scr["gmid"] = []
    for p in range(HEADS):
        first, second = (ny, zh_n) if p < 2 else (zh_n, ny)
        a, b, c = full[p]
        scr["xr"].append([vm(first - 1, second), vm(second - 1)])
        scr["gr"].append([vm(a - 1, b, c), vm(b - 1, c), vm(c - 1)])
        scr["gmid"].append([vm(b, c), vm(c)])
    return scr


def local(
    geom,
    node_cache,
    node_hidden,
    node_slot,
    parent,
    child_query,
    child_kv,
    routes,
    gate_w,
    w_gate,
    w_up,
    w_down,
):
    features = w_gate.shape[1]
    smem = pl.BlockSpec(memory_space=pltpu.SMEM)
    vmem = pl.BlockSpec(memory_space=pltpu.VMEM)
    hbm = pl.BlockSpec(memory_space=pl.ANY)
    return pl.pallas_call(
        functools.partial(kernel, geom),
        out_shape=jax.ShapeDtypeStruct(child_query.shape[:2] + (HEADS * LANES,), BF),
        in_specs=[smem] * 3 + [vmem] * 4 + [hbm] * 4,
        out_specs=vmem,
        scratch_shapes=[scratch_of(geom, features)],
        compiler_params=pltpu.CompilerParams(
            collective_id=0, has_side_effects=True, vmem_limit_bytes=58 * 1024 * 1024
        ),
    )(
        node_slot,
        routes.transpose(0, 2, 1),
        gate_w.transpose(0, 2, 1),
        parent.reshape(1, -1),
        child_query.transpose(0, 2, 1, 3),
        child_kv,
        node_hidden,
        node_cache,
        w_gate,
        w_up,
        w_down,
    )


def solution(mesh):
    leaves, experts, mp = mesh.shape["leaf"], mesh.shape["expert"], mesh.shape["mp"]
    geom = (experts // 2, NY, leaves // NY, mp)
    in_specs = (
        P("leaf", "expert", None, None, None),
        P("leaf", ("expert", "mp")),
        P(),
        P(),
        P("leaf", None, ("expert", "mp"), None),
        P("leaf", "expert", None, None, None),
        P("leaf", None, None),
        P("leaf", None, None),
        P("expert", None, ("leaf", "mp")),
        P("expert", None, ("leaf", "mp")),
        P("expert", ("leaf", "mp"), None),
    )
    out_specs = P("leaf", None, ("expert", "mp"))
    return jax.shard_map(
        functools.partial(local, geom),
        mesh=mesh,
        in_specs=in_specs,
        out_specs=out_specs,
        check_vma=False,
    )
```

```python
import functools
import itertools

import jax
import jax.numpy as jnp
from jax import lax
from jax.experimental import pallas as pl
from jax.experimental.pallas import tpu as pltpu
from jax.sharding import PartitionSpec as P

F32 = jnp.float32
BF = jnp.bfloat16
SENDS = 40
RECVS = 56
LANES = 128
TOK = 8
HEADS = 3
NY = 8


class Ring:
    def __init__(self, size, me, device):
        self.size = size
        self.me = me
        self.device = device

    def at(self, offset):
        return lax.rem(self.me + offset + 2 * self.size, self.size)

    def near_first(self):
        return sorted(range(1, self.size), key=lambda k: (min(k, self.size - k), k))

    def far_first(self):
        return self.near_first()[::-1]


def interleave(jobs):
    jobs = list(jobs)
    while jobs:
        alive = []
        for job in jobs:
            try:
                next(job)
                alive.append(job)
            except StopIteration:
                pass
        jobs = alive


def kernel(
    geom,
    slot_ref,
    routes_ref,
    gate_ref,
    parent_ref,
    query_ref,
    kv_ref,
    hid_ref,
    cache_ref,
    wg_ref,
    wu_ref,
    wd_ref,
    out_ref,
    scr,
):
    nx, ny, zh_n, zl_n = geom
    nz = zh_n * zl_n
    leaves = zh_n * ny
    tokens = leaves * TOK
    width = HEADS * LANES

    leaf = lax.axis_index("leaf")
    expert = lax.axis_index("expert")
    mp = lax.axis_index("mp")
    y = lax.rem(leaf, ny)
    zh = lax.div(leaf, ny)
    x = lax.div(expert, 2)
    core = lax.rem(expert, 2)
    z = zh * zl_n + mp

    def dev_x(k):
        return {"leaf": leaf, "expert": k * 2 + core, "mp": mp}

    def dev_y(k):
        return {"leaf": zh * ny + k, "expert": expert, "mp": mp}

    def dev_zh(k):
        return {"leaf": k * ny + y, "expert": expert, "mp": mp}

    def dev_z(k):
        return {
            "leaf": lax.div(k, zl_n) * ny + y,
            "expert": expert,
            "mp": lax.rem(k, zl_n),
        }

    sibling = {"leaf": leaf, "expert": x * 2 + (1 - core), "mp": mp}
    rx = Ring(nx, x, dev_x)
    ry = Ring(ny, y, dev_y)
    rz = Ring(nz, z, dev_z)
    rzh = Ring(zh_n, zh, dev_zh)

    send_sems, recv_sems, load_sems = scr["send"], scr["recv"], scr["load"]
    next_send = itertools.count()
    next_recv = itertools.count()
    pending = []

    def transfer(src, dst, device, send, recv):
        return pltpu.make_async_remote_copy(
            src_ref=src,
            dst_ref=dst,
            send_sem=send_sems.at[send],
            recv_sem=recv_sems.at[recv],
            device_id=device,
            device_id_type=pl.DeviceIdType.MESH,
        )

    def arrive(ref, recv):
        transfer(ref, ref, sibling, 0, recv).wait_recv()

    def gather(buf, ring, got=None):
        others = buf.at[pl.ds(0, ring.size - 1)]
        send = next(next_send)
        recvs = {k: next(next_recv) for k in range(1, ring.size if got else 2)}
        for k in ring.far_first():
            mine = buf.at[ring.me]
            transfer(mine, mine, ring.device(ring.at(k)), send, recvs[k if got else 1]).start()
        pending.append((others, send))
        yield
        if got is None:
            arrive(others, recvs[1])
        else:
            for k in ring.near_first():
                index = ring.at(-k)
                arrive(buf.at[index], recvs[k])
                got(index)

    def scatter(h, r, ring, finish):
        send, recv = next(next_send), next(next_recv)
        for k in ring.far_first():
            to = ring.at(k)
            transfer(h.at[to], r.at[k - 1], ring.device(to), send, recv).start()
        pending.append((r, send))
        yield
        arrive(r, recv)
        total = h[ring.me].astype(F32)
        for k in range(ring.size - 1):
            total = total + r[k].astype(F32)
        finish(total)

    barrier = pltpu.get_barrier_semaphore()
    partners = [sibling]
    for ring in (rx, ry, rz):
        partners += [ring.device(ring.at(k)) for k in range(1, ring.size)]
    for partner in partners:
        pl.semaphore_signal(barrier, inc=1, device_id=partner, device_id_type=pl.DeviceIdType.MESH)

    loads = [
        pltpu.make_async_copy(wg_ref.at[0], scr["wgu"].at[:, pl.ds(0, LANES)], load_sems.at[0]),
        pltpu.make_async_copy(wu_ref.at[0], scr["wgu"].at[:, pl.ds(LANES, LANES)], load_sems.at[1]),
        pltpu.make_async_copy(cache_ref.at[0, 0], scr["cache"], load_sems.at[2]),
    ]
    span = zl_n * width

    def down_block(i, which):
        off = pl.multiple_of((i * 2 + which) * span, LANES)
        return wd_ref.at[0, :, pl.ds(off, span)]

    loads += [
        pltpu.make_async_copy(
            down_block(i, core),
            scr["wd"].at[pl.ds(0, LANES), pl.ds(i * span, span)],
            load_sems.at[3 + i],
        )
        for i in range(nx)
    ]
    for c in loads:
        c.start()

    abuf, bbuf = scr["abuf"], scr["bbuf"]
    row = lax.broadcasted_iota(jnp.int32, (TOK, LANES), 0)
    lane = lax.broadcasted_iota(jnp.int32, (TOK, LANES), 1)
    weight = jnp.zeros((TOK, LANES), F32)
    for t in range(TOK):
        w = jnp.float32(0.0)
        for k in range(2):
            w += jnp.where(
                routes_ref[t // 4, k, t % 4] == expert, gate_ref[t // 4, k, t % 4], 0.0
            )
        weight = jnp.where(row == t, w, weight)
    high = weight.astype(BF).astype(F32)
    for h in range(HEADS):
        abuf[y, zh, pl.ds(h * TOK, TOK)] = (
            query_ref[:, h].astype(F32).reshape(TOK, LANES).astype(BF)
        )
    bbuf[zh, y, pl.ds(2 * TOK, TOK)] = jnp.where(
        lane == 0, high, jnp.where(lane == 1, weight - high, 0.0)
    ).astype(BF)
    for k in range(2):
        part = kv_ref[:, 0, k].astype(F32).reshape(TOK, LANES)
        bbuf[zh, y, pl.ds(k * TOK, TOK)] = part.astype(BF)

    pl.semaphore_wait(barrier, len(partners))

    other = scr["wd"].at[pl.ds(LANES, LANES)]
    wd_send, wd_recv = next(next_send), next(next_recv)
    for i in range(nx):
        transfer(
            down_block(i, 1 - core), other.at[:, pl.ds(i * span, span)], sibling, wd_send, wd_recv
        ).start()
    pending.append((other, wd_send))

    def gather_a():
        yield from gather(abuf.at[y], rzh)
        yield from gather(abuf, ry)

    def gather_b():
        yield from gather(bbuf.at[zh], ry)
        yield from gather(bbuf, rzh)

    interleave([gather_a(), gather_b()])

    def rows_a(k):
        return jnp.concatenate(
            [
                abuf[:, i, pl.ds(k * TOK, TOK)].astype(F32).reshape(ny * TOK, LANES)
                for i in range(zh_n)
            ],
            axis=0,
        )

    def rows_b(k):
        return bbuf[:, :, pl.ds(k * TOK, TOK)].astype(F32).reshape(tokens, LANES)

    new_k = rows_b(0).astype(BF)
    new_v = rows_b(1).astype(BF)
    loads[2].wait()
    old_k = scr["cache"][0]
    old_v = scr["cache"][1]
    contract = (((1,), (1,)), ((), ()))
    row_id = lax.broadcasted_iota(jnp.int32, (tokens, tokens), 0)
    col_id = lax.broadcasted_iota(jnp.int32, (tokens, tokens), 1)
    allowed = (row_id // 4 == col_id // 4) & (col_id <= row_id)
    scale = 1.0 / LANES**0.5
    node = jnp.int32(0)
    for k in range(leaves):
        node += jnp.where(slot_ref[k] == leaf, k, 0)
    children = leaves * 2
    token_child = lax.broadcasted_iota(jnp.int32, (tokens, children), 0) // 4
    child_id = lax.broadcasted_iota(jnp.int32, (tokens, children), 1)
    here_row = (token_child == child_id) & (parent_ref[...] == node)
    mine = jnp.sum(jnp.where(here_row, 1.0, 0.0), axis=1, keepdims=True)
    xp = [scr["xp0"], scr["xp1"], scr["xp2"]]
    for p in range(HEADS):
        q = rows_a(p).astype(BF)
        s_old = lax.dot_general(q, old_k, contract, preferred_element_type=F32) * scale
        s_new = lax.dot_general(q, new_k, contract, preferred_element_type=F32) * scale
        s_new = jnp.where(allowed, s_new, -1e30)
        top = jnp.maximum(
            jnp.max(s_old, axis=1, keepdims=True), jnp.max(s_new, axis=1, keepdims=True)
        )
        e_old = jnp.exp(s_old - top)
        e_new = jnp.exp(s_new - top)
        total = jnp.sum(e_old, axis=1, keepdims=True) + jnp.sum(e_new, axis=1, keepdims=True)
        inv = 1.0 / total
        attn = jnp.dot((e_old * inv).astype(BF), old_v, preferred_element_type=F32)
        attn += jnp.dot((e_new * inv).astype(BF), new_v, preferred_element_type=F32)
        row = hid_ref[:, pl.ds(p * LANES, LANES)].astype(F32)
        here = jnp.where(mine > 0.5, attn + row, 0.0)
        here = here.reshape(zh_n, ny, TOK, LANES)
        if p < 2:
            for i in range(zh_n):
                xp[p][:, i] = here[i].astype(BF)
        else:
            xp[p][...] = here.astype(BF)

    own = [scr["own0"], scr["own1"], scr["own2"]]
    xr = scr["xr"]
    mids = scr["xmid"]
    xs = scr["xs"]

    def own_at(p):
        if p == 0:
            return own[0].at[z, y]
        if p == 1:
            return own[1].at[y, x]
        return own[2].at[x, z]

    def home(p):
        first, second = (ry, rzh) if p < 2 else (rzh, ry)

        def keep(v):
            mids[p][...] = v.astype(BF)

        yield from scatter(xp[p], xr[p][0], first, keep)

        def final(v):
            w = v.astype(BF)
            xs[p] = w
            if p == 0:
                own[0][z, y, x] = w
            elif p == 1:
                own[1][y, x, z] = w
            else:
                own[2][x, z, y] = w

        yield from scatter(mids[p], xr[p][1], second, final)

    interleave([home(p) for p in range(HEADS)])

    sib = [scr["sib0"], scr["sib1"], scr["sib2"]]
    d2d = []
    orders = [(rx, ry, rz), (rz, rx, ry), (ry, rz, rx)]

    def everywhere(p):
        one, two, three = orders[p]
        yield from gather(own_at(p), one)
        last = own[p].at[three.me]
        yield from gather(last, two)

        send, recv = next(next_send), next(next_recv)

        def forward(index):
            transfer(own[p].at[index], sib[p].at[index], sibling, send, recv).start()

        pending.append((own[p], send))
        d2d.append((sib[p], recv))
        forward(three.me)
        yield from gather(own[p], three, forward)

    interleave([everywhere(p) for p in range(HEADS)])

    def tiles(refs, p, xi, m, i):
        zi = i * zl_n + m
        if p == 0:
            return refs[0].at[zi, :, xi]
        if p == 1:
            return refs[1].at[:, xi, zi]
        return refs[2].at[xi, zi]

    acc = scr["acc"]
    acc[...] = jnp.zeros_like(acc)
    for c in loads[:2] + loads[3:]:
        c.wait()
    blocks = nx * zl_n

    def up(refs, which):
        @pl.loop(0, blocks)
        def _(j):
            xi, m = lax.div(j, zl_n), lax.rem(j, zl_n)
            cols = []
            for p in range(HEADS):
                cols.append(
                    jnp.concatenate(
                        [
                            tiles(refs, p, xi, m, i)[...].astype(F32).reshape(ny * TOK, LANES)
                            for i in range(zh_n)
                        ],
                        axis=0,
                    ).astype(BF)
                )
            rows = jnp.concatenate(cols, axis=1)
            off = pl.multiple_of(((xi * 2 + which) * zl_n + m) * width, LANES)
            acc[...] += jnp.dot(rows, scr["wgu"][pl.ds(off, width), :], preferred_element_type=F32)

    up(own, core)
    for ref, recv in d2d:
        arrive(ref, recv)
    up(sib, 1 - core)

    gates = rows_b(2)
    gate = gates[:, 0:1] + gates[:, 1:2]
    g = acc[:, pl.ds(0, LANES)]
    u = acc[:, pl.ds(LANES, LANES)]
    units = (g * (1.0 / (1.0 + jnp.exp(-g))) * u).astype(BF).astype(F32)
    mine_units, other_units = scr["units"], scr["units_other"]
    mine_units[...] = (units * gate).astype(BF)
    u_send, u_recv = next(next_send), next(next_recv)
    transfer(mine_units, other_units, sibling, u_send, u_recv).start()
    pending.append((other_units, u_send))
    ho = [scr["ho0"], scr["ho1"], scr["ho2"]]
    arrive(other, wd_recv)
    arrive(other_units, u_recv)

    def down(parts):
        count = len(parts) * LANES

        @pl.loop(0, blocks)
        def _(j):
            xi, m = lax.div(j, zl_n), lax.rem(j, zl_n)
            both = jnp.concatenate([mine_units[...], other_units[...]], axis=1)
            off = pl.multiple_of(j * width + parts[0] * LANES, LANES)
            o = jnp.dot(both, scr["wd"][:, pl.ds(off, count)], preferred_element_type=F32)
            for k, p in enumerate(parts):
                part = o[:, k * LANES : (k + 1) * LANES].reshape(zh_n, ny, TOK, LANES)
                for i in range(zh_n):
                    tiles(ho, p, xi, m, i)[...] = part[i].astype(BF)

    gr = scr["gr"]
    gmid = scr["gmid"]

    def back(p):
        one, two, three = orders[p]
        if p == 0:
            down((0, 1))
        if p == 2:
            down((2,))

        def keep(level):
            def write(v):
                gmid[p][level][...] = v.astype(BF)

            return write

        yield from scatter(ho[p], gr[p][0], three, keep(0))
        yield from scatter(gmid[p][0], gr[p][1], two, keep(1))

        def final(v):
            w = (xs[p].astype(F32) + v).astype(BF)
            for c in range(2):
                out_ref[c, :, pl.ds(p * LANES, LANES)] = w[c * 4 : c * 4 + 4]

        yield from scatter(gmid[p][1], gr[p][2], one, final)

    interleave([back(p) for p in range(HEADS)])

    for ref, send in pending:
        transfer(ref, ref, sibling, send, 0).wait_send()


def scratch_of(geom, features):
    nx, ny, zh_n, zl_n = geom
    nz = zh_n * zl_n
    tokens = zh_n * ny * TOK
    tile = (TOK, LANES)
    vm = lambda *shape: pltpu.VMEM(shape + tile, BF)
    full = [(nz, ny, nx), (ny, nx, nz), (nx, nz, ny)]
    scr = {
        "send": pltpu.SemaphoreType.DMA((SENDS,)),
        "recv": pltpu.SemaphoreType.DMA((RECVS,)),
        "load": pltpu.SemaphoreType.DMA((3 + nx,)),
        "cache": pltpu.VMEM((2, 256, LANES), BF),
        "wgu": pltpu.VMEM((features, 2 * LANES), BF),
        "wd": pltpu.VMEM((2 * LANES, features // 2), BF),
        "abuf": pltpu.VMEM((ny, zh_n, HEADS * TOK, LANES), BF),
        "bbuf": pltpu.VMEM((zh_n, ny, 3 * TOK, LANES), BF),
        "xs": vm(HEADS),
        "acc": pltpu.VMEM((tokens, 2 * LANES), F32),
        "units": pltpu.VMEM((tokens, LANES), BF),
        "units_other": pltpu.VMEM((tokens, LANES), BF),
    }
    for p in range(HEADS):
        a, b, c = full[p]
        for name in ("own", "sib", "ho"):
            scr[name + str(p)] = vm(a, b, c)
        scr["xp" + str(p)] = vm(ny, zh_n) if p < 2 else vm(zh_n, ny)
    scr["xmid"] = [vm(zh_n), vm(zh_n), vm(ny)]
    scr["xr"] = []
    scr["gr"] = []
    scr["gmid"] = []
    for p in range(HEADS):
        first, second = (ny, zh_n) if p < 2 else (zh_n, ny)
        a, b, c = full[p]
        scr["xr"].append([vm(first - 1, second), vm(second - 1)])
        scr["gr"].append([vm(a - 1, b, c), vm(b - 1, c), vm(c - 1)])
        scr["gmid"].append([vm(b, c), vm(c)])
    return scr


def local(
    geom,
    node_cache,
    node_hidden,
    node_slot,
    parent,
    child_query,
    child_kv,
    routes,
    gate_w,
    w_gate,
    w_up,
    w_down,
):
    features = w_gate.shape[1]
    smem = pl.BlockSpec(memory_space=pltpu.SMEM)
    vmem = pl.BlockSpec(memory_space=pltpu.VMEM)
    hbm = pl.BlockSpec(memory_space=pl.ANY)
    return pl.pallas_call(
        functools.partial(kernel, geom),
        out_shape=jax.ShapeDtypeStruct(child_query.shape[:2] + (HEADS * LANES,), BF),
        in_specs=[smem] * 3 + [vmem] * 4 + [hbm] * 4,
        out_specs=vmem,
        scratch_shapes=[scratch_of(geom, features)],
        compiler_params=pltpu.CompilerParams(
            collective_id=0, has_side_effects=True, vmem_limit_bytes=58 * 1024 * 1024
        ),
    )(
        node_slot,
        routes.transpose(0, 2, 1),
        gate_w.transpose(0, 2, 1),
        parent.reshape(1, -1),
        child_query.transpose(0, 2, 1, 3),
        child_kv,
        node_hidden,
        node_cache,
        w_gate,
        w_up,
        w_down,
    )


def solution(mesh):
    leaves, experts, mp = mesh.shape["leaf"], mesh.shape["expert"], mesh.shape["mp"]
    geom = (experts // 2, NY, leaves // NY, mp)
    in_specs = (
        P("leaf", "expert", None, None, None),
        P("leaf", ("expert", "mp")),
        P(),
        P(),
        P("leaf", None, ("expert", "mp"), None),
        P("leaf", "expert", None, None, None),
        P("leaf", None, None),
        P("leaf", None, None),
        P("expert", None, ("leaf", "mp")),
        P("expert", None, ("leaf", "mp")),
        P("expert", ("leaf", "mp"), None),
    )
    out_specs = P("leaf", None, ("expert", "mp"))
    return jax.shard_map(
        functools.partial(local, geom),
        mesh=mesh,
        in_specs=in_specs,
        out_specs=out_specs,
        check_vma=False,
    )
```

```python
import functools
import itertools

import jax
import jax.numpy as jnp
from jax import lax
from jax.experimental import pallas as pl
from jax.experimental.pallas import tpu as pltpu
from jax.sharding import PartitionSpec as P

F32 = jnp.float32
BF = jnp.bfloat16
SENDS = 44
RECVS = 62
LANES = 128
TOK = 8
HEADS = 3
NY = 8


class Ring:
    def __init__(self, size, me, device):
        self.size = size
        self.me = me
        self.device = device

    def at(self, offset):
        return lax.rem(self.me + offset + 2 * self.size, self.size)

    def near_first(self):
        return sorted(range(1, self.size), key=lambda k: (min(k, self.size - k), k))

    def far_first(self):
        return self.near_first()[::-1]


def interleave(jobs):
    jobs = list(jobs)
    while jobs:
        alive = []
        for job in jobs:
            try:
                next(job)
                alive.append(job)
            except StopIteration:
                pass
        jobs = alive


def kernel(
    geom,
    slot_ref,
    routes_ref,
    gate_ref,
    parent_ref,
    query_ref,
    kv_ref,
    hid_ref,
    cache_ref,
    wg_ref,
    wu_ref,
    wd_ref,
    out_ref,
    scr,
):
    nx, ny, zh_n, zl_n = geom
    nz = zh_n * zl_n
    cut_y, cut_z = cuts_of(geom)
    leaves = zh_n * ny
    tokens = leaves * TOK
    width = HEADS * LANES

    leaf = lax.axis_index("leaf")
    expert = lax.axis_index("expert")
    mp = lax.axis_index("mp")
    y = lax.rem(leaf, ny)
    zh = lax.div(leaf, ny)
    x = lax.div(expert, 2)
    core = lax.rem(expert, 2)
    z = zh * zl_n + mp

    def dev_x(k):
        return {"leaf": leaf, "expert": k * 2 + core, "mp": mp}

    def dev_y(k):
        return {"leaf": zh * ny + k, "expert": expert, "mp": mp}

    def dev_zh(k):
        return {"leaf": k * ny + y, "expert": expert, "mp": mp}

    def dev_z(k):
        return {
            "leaf": lax.div(k, zl_n) * ny + y,
            "expert": expert,
            "mp": lax.rem(k, zl_n),
        }

    sibling = {"leaf": leaf, "expert": x * 2 + (1 - core), "mp": mp}
    rx = Ring(nx, x, dev_x)
    ry = Ring(ny, y, dev_y)
    rz = Ring(nz, z, dev_z)
    rzh = Ring(zh_n, zh, dev_zh)

    send_sems, recv_sems, load_sems = scr["send"], scr["recv"], scr["load"]
    next_send = itertools.count()
    next_recv = itertools.count()
    pending = []

    def transfer(src, dst, device, send, recv):
        return pltpu.make_async_remote_copy(
            src_ref=src,
            dst_ref=dst,
            send_sem=send_sems.at[send],
            recv_sem=recv_sems.at[recv],
            device_id=device,
            device_id_type=pl.DeviceIdType.MESH,
        )

    def arrive(ref, recv):
        transfer(ref, ref, sibling, 0, recv).wait_recv()

    def gather(buf, ring, got=None):
        others = buf.at[pl.ds(0, ring.size - 1)]
        send = next(next_send)
        recvs = {k: next(next_recv) for k in range(1, ring.size if got else 2)}
        for k in ring.far_first():
            mine = buf.at[ring.me]
            transfer(mine, mine, ring.device(ring.at(k)), send, recvs[k if got else 1]).start()
        pending.append((others, send))
        yield
        if got is None:
            arrive(others, recvs[1])
        else:
            for k in ring.near_first():
                index = ring.at(-k)
                arrive(buf.at[index], recvs[k])
                got(index)

    def scatter(h, r, ring, finish):
        send, recv = next(next_send), next(next_recv)
        for k in ring.far_first():
            to = ring.at(k)
            transfer(h.at[to], r.at[k - 1], ring.device(to), send, recv).start()
        pending.append((r, send))
        yield
        arrive(r, recv)
        total = h[ring.me].astype(F32)
        for k in range(ring.size - 1):
            total = total + r[k].astype(F32)
        finish(total)

    inputs = [slot_ref, routes_ref, gate_ref, parent_ref, query_ref, kv_ref, hid_ref]
    held = scr["held"]
    small = [
        pltpu.make_async_copy(src, dst, scr["small"].at[i])
        for i, (src, dst) in enumerate(zip(inputs, held))
    ]
    for c in small:
        c.start()

    barrier = pltpu.get_barrier_semaphore()
    partners = [sibling]
    for ring in (rx, ry, rz):
        partners += [ring.device(ring.at(k)) for k in range(1, ring.size)]
    for partner in partners:
        pl.semaphore_signal(barrier, inc=1, device_id=partner, device_id_type=pl.DeviceIdType.MESH)

    loads = [
        pltpu.make_async_copy(wg_ref.at[0], scr["wgu"].at[:, pl.ds(0, LANES)], load_sems.at[0]),
        pltpu.make_async_copy(wu_ref.at[0], scr["wgu"].at[:, pl.ds(LANES, LANES)], load_sems.at[1]),
        pltpu.make_async_copy(cache_ref.at[0, 0], scr["cache"], load_sems.at[2]),
    ]
    span = zl_n * width

    def down_block(i, which):
        off = pl.multiple_of((i * 2 + which) * span, LANES)
        return wd_ref.at[0, :, pl.ds(off, span)]

    loads += [
        pltpu.make_async_copy(
            down_block(i, core),
            scr["wd"].at[pl.ds(0, LANES), pl.ds(i * span, span)],
            load_sems.at[3 + i],
        )
        for i in range(nx)
    ]
    for c in loads:
        c.start()

    for c in small:
        c.wait()
    slot_ref, routes_ref, gate_ref, parent_ref, query_ref, kv_ref, hid_ref = held
    abuf, bbuf = scr["abuf"], scr["bbuf"]
    row = lax.broadcasted_iota(jnp.int32, (TOK, LANES), 0)
    lane = lax.broadcasted_iota(jnp.int32, (TOK, LANES), 1)
    weight = jnp.zeros((TOK, LANES), F32)
    for t in range(TOK):
        w = jnp.float32(0.0)
        for k in range(2):
            w += jnp.where(
                routes_ref[t // 4, k, t % 4] == expert, gate_ref[t // 4, k, t % 4], 0.0
            )
        weight = jnp.where(row == t, w, weight)
    high = weight.astype(BF).astype(F32)
    for h in range(HEADS):
        abuf[y, zh, pl.ds(h * TOK, TOK)] = (
            query_ref[:, h].astype(F32).reshape(TOK, LANES).astype(BF)
        )
    bbuf[zh, y, pl.ds(2 * TOK, TOK)] = jnp.where(
        lane == 0, high, jnp.where(lane == 1, weight - high, 0.0)
    ).astype(BF)
    for k in range(2):
        part = kv_ref[:, 0, k].astype(F32).reshape(TOK, LANES)
        bbuf[zh, y, pl.ds(k * TOK, TOK)] = part.astype(BF)

    pl.semaphore_wait(barrier, len(partners))

    other = scr["wd"].at[pl.ds(LANES, LANES)]
    wd_send, wd_recv = next(next_send), next(next_recv)
    for i in range(nx):
        transfer(
            down_block(i, 1 - core), other.at[:, pl.ds(i * span, span)], sibling, wd_send, wd_recv
        ).start()
    pending.append((other, wd_send))

    def gather_a():
        yield from gather(abuf.at[y], rzh)
        yield from gather(abuf, ry)

    def gather_b():
        yield from gather(bbuf.at[zh], ry)
        yield from gather(bbuf, rzh)

    interleave([gather_a(), gather_b()])

    def rows_a(k):
        return jnp.concatenate(
            [
                abuf[:, i, pl.ds(k * TOK, TOK)].astype(F32).reshape(ny * TOK, LANES)
                for i in range(zh_n)
            ],
            axis=0,
        )

    def rows_b(k):
        return bbuf[:, :, pl.ds(k * TOK, TOK)].astype(F32).reshape(tokens, LANES)

    new_k = rows_b(0).astype(BF)
    new_v = rows_b(1).astype(BF)
    loads[2].wait()
    old_k = scr["cache"][0]
    old_v = scr["cache"][1]
    contract = (((1,), (1,)), ((), ()))
    row_id = lax.broadcasted_iota(jnp.int32, (tokens, tokens), 0)
    col_id = lax.broadcasted_iota(jnp.int32, (tokens, tokens), 1)
    allowed = (row_id // 4 == col_id // 4) & (col_id <= row_id)
    scale = 1.0 / LANES**0.5
    node = jnp.int32(0)
    for k in range(leaves):
        node += jnp.where(slot_ref[k] == leaf, k, 0)
    children = leaves * 2
    token_child = lax.broadcasted_iota(jnp.int32, (tokens, children), 0) // 4
    child_id = lax.broadcasted_iota(jnp.int32, (tokens, children), 1)
    here_row = (token_child == child_id) & (parent_ref[...] == node)
    mine = jnp.sum(jnp.where(here_row, 1.0, 0.0), axis=1, keepdims=True)
    xp = [scr["xp0"], scr["xp1"], scr["xp2"]]
    for p in range(HEADS):
        q = rows_a(p).astype(BF)
        s_old = lax.dot_general(q, old_k, contract, preferred_element_type=F32) * scale
        s_new = lax.dot_general(q, new_k, contract, preferred_element_type=F32) * scale
        s_new = jnp.where(allowed, s_new, -1e30)
        top = jnp.maximum(
            jnp.max(s_old, axis=1, keepdims=True), jnp.max(s_new, axis=1, keepdims=True)
        )
        e_old = jnp.exp(s_old - top)
        e_new = jnp.exp(s_new - top)
        total = jnp.sum(e_old, axis=1, keepdims=True) + jnp.sum(e_new, axis=1, keepdims=True)
        inv = 1.0 / total
        attn = jnp.dot((e_old * inv).astype(BF), old_v, preferred_element_type=F32)
        attn += jnp.dot((e_new * inv).astype(BF), new_v, preferred_element_type=F32)
        row = hid_ref[:, pl.ds(p * LANES, LANES)].astype(F32)
        here = jnp.where(mine > 0.5, attn + row, 0.0)
        here = here.reshape(zh_n, ny, TOK, LANES)
        if p < 2:
            for i in range(zh_n):
                xp[p][:, i] = here[i].astype(BF)
        else:
            xp[p][...] = here.astype(BF)

    own = scr["own"]
    start = scr["start"]
    xr = scr["xr"]
    mids = scr["xmid"]
    xs = scr["xs"]
    firsts = (ry, rz, ry)

    def home(p):
        first, second = (ry, rzh) if p < 2 else (rzh, ry)

        def keep(v):
            mids[p][...] = v.astype(BF)

        yield from scatter(xp[p], xr[p][0], first, keep)

        def final(v):
            w = v.astype(BF)
            xs[p] = w
            start[p][firsts[p].me] = w

        yield from scatter(mids[p], xr[p][1], second, final)

    interleave([home(p) for p in range(HEADS)])

    sib = scr["sib"]
    d2d = []
    rings = {"x": rx, "y": ry, "z": rz}
    pieces = pieces_of(geom)

    interleave([gather(start[p], firsts[p]) for p in range(HEADS)])

    def everywhere(k):
        p, low, many, two, three = pieces[k]
        two, three = rings[two], rings[three]
        own[k][three.me, two.me] = start[p][pl.ds(low, many)]
        yield from gather(own[k].at[three.me], two)

        send, recv = next(next_send), next(next_recv)

        def forward(index):
            transfer(own[k].at[index], sib[k].at[index], sibling, send, recv).start()

        pending.append((own[k], send))
        d2d.append((sib[k], recv))
        forward(three.me)
        yield from gather(own[k], three, forward)

    interleave([everywhere(k) for k in range(len(pieces))])

    def tiles(refs, p, xi, m, i):
        zi = i * zl_n + m
        if p == 0:
            return [(refs[0].at[zi, xi], 0, cut_y), (refs[1].at[xi, zi], cut_y, ny - cut_y)]
        if p == 1:
            if i * zl_n < cut_z:
                return [(refs[2].at[:, xi, zi], 0, ny)]
            return [(refs[3].at[xi, :, zi - cut_z], 0, ny)]
        return [(refs[4].at[xi, zi], 0, ny)]

    def rows_of(refs, p, xi, m, i):
        parts = [ref[...].astype(F32) for ref, _, _ in tiles(refs, p, xi, m, i)]
        part = parts[0] if len(parts) == 1 else jnp.concatenate(parts, axis=0)
        return part.reshape(ny * TOK, LANES)

    acc = scr["acc"]
    acc[...] = jnp.zeros_like(acc)
    for c in loads[:2] + loads[3:]:
        c.wait()
    blocks = nx * zl_n

    def up(refs, which):
        @pl.loop(0, blocks)
        def _(j):
            xi, m = lax.div(j, zl_n), lax.rem(j, zl_n)
            cols = []
            for p in range(HEADS):
                cols.append(
                    jnp.concatenate(
                        [rows_of(refs, p, xi, m, i) for i in range(zh_n)],
                        axis=0,
                    ).astype(BF)
                )
            rows = jnp.concatenate(cols, axis=1)
            off = pl.multiple_of(((xi * 2 + which) * zl_n + m) * width, LANES)
            acc[...] += jnp.dot(rows, scr["wgu"][pl.ds(off, width), :], preferred_element_type=F32)

    up(own, core)
    for ref, recv in d2d:
        arrive(ref, recv)
    up(sib, 1 - core)

    gates = rows_b(2)
    gate = gates[:, 0:1] + gates[:, 1:2]
    g = acc[:, pl.ds(0, LANES)]
    u = acc[:, pl.ds(LANES, LANES)]
    units = (g * (1.0 / (1.0 + jnp.exp(-g))) * u).astype(BF).astype(F32)
    mine_units, other_units = scr["units"], scr["units_other"]
    mine_units[...] = (units * gate).astype(BF)
    u_send, u_recv = next(next_send), next(next_recv)
    transfer(mine_units, other_units, sibling, u_send, u_recv).start()
    pending.append((other_units, u_send))
    ho = scr["ho"]
    arrive(other, wd_recv)
    arrive(other_units, u_recv)

    def down(parts):
        count = len(parts) * LANES

        @pl.loop(0, blocks)
        def _(j):
            xi, m = lax.div(j, zl_n), lax.rem(j, zl_n)
            both = jnp.concatenate([mine_units[...], other_units[...]], axis=1)
            off = pl.multiple_of(j * width + parts[0] * LANES, LANES)
            o = jnp.dot(both, scr["wd"][:, pl.ds(off, count)], preferred_element_type=F32)
            for k, p in enumerate(parts):
                part = o[:, k * LANES : (k + 1) * LANES].reshape(zh_n, ny, TOK, LANES)
                for i in range(zh_n):
                    for ref, low, many in tiles(ho, p, xi, m, i):
                        ref[...] = part[i][low : low + many].astype(BF)

    gr, gmid, ends, er = scr["gr"], scr["gmid"], scr["ends"], scr["er"]

    def back(k):
        p, low, many, two, three = pieces[k]
        if k == 0:
            down((0, 1))
        if p == 2:
            down((2,))

        def keep(v):
            gmid[k][...] = v.astype(BF)

        def end(v):
            ends[p][pl.ds(low, many)] = v.astype(BF)

        yield from scatter(ho[k], gr[k][0], rings[three], keep)
        yield from scatter(gmid[k], gr[k][1], rings[two], end)

    interleave([back(k) for k in range(len(pieces))])

    def last(p):
        def final(v):
            w = (xs[p].astype(F32) + v).astype(BF)
            for c in range(2):
                out_ref[c, :, pl.ds(p * LANES, LANES)] = w[c * 4 : c * 4 + 4]

        yield from scatter(ends[p], er[p], firsts[p], final)

    interleave([last(p) for p in range(HEADS)])

    for ref, send in pending:
        transfer(ref, ref, sibling, send, 0).wait_send()


def cuts_of(geom):
    nx, ny, zh_n, zl_n = geom
    return ny * 3 // 4, zh_n * 3 // 4 * zl_n


def pieces_of(geom):
    nx, ny, zh_n, zl_n = geom
    nz = zh_n * zl_n
    cut_y, cut_z = cuts_of(geom)
    return [
        (0, 0, cut_y, "x", "z"),
        (0, cut_y, ny - cut_y, "z", "x"),
        (1, 0, cut_z, "x", "y"),
        (1, cut_z, nz - cut_z, "y", "x"),
        (2, 0, ny, "z", "x"),
    ]


def scratch_of(geom, features, held):
    nx, ny, zh_n, zl_n = geom
    nz = zh_n * zl_n
    tokens = zh_n * ny * TOK
    tile = (TOK, LANES)
    vm = lambda *shape: pltpu.VMEM(shape + tile, BF)
    size = {"x": nx, "y": ny, "z": nz}
    pieces = pieces_of(geom)
    scr = {
        "send": pltpu.SemaphoreType.DMA((SENDS,)),
        "recv": pltpu.SemaphoreType.DMA((RECVS,)),
        "held": held,
        "small": pltpu.SemaphoreType.DMA((len(held),)),
        "load": pltpu.SemaphoreType.DMA((3 + nx,)),
        "cache": pltpu.VMEM((2, 256, LANES), BF),
        "wgu": pltpu.VMEM((features, 2 * LANES), BF),
        "wd": pltpu.VMEM((2 * LANES, features // 2), BF),
        "abuf": pltpu.VMEM((ny, zh_n, HEADS * TOK, LANES), BF),
        "bbuf": pltpu.VMEM((zh_n, ny, 3 * TOK, LANES), BF),
        "xs": vm(HEADS),
        "acc": pltpu.VMEM((tokens, 2 * LANES), F32),
        "units": pltpu.VMEM((tokens, LANES), BF),
        "units_other": pltpu.VMEM((tokens, LANES), BF),
    }
    for p in range(HEADS):
        scr["xp" + str(p)] = vm(ny, zh_n) if p < 2 else vm(zh_n, ny)
    for name in ("own", "sib", "ho"):
        scr[name] = [vm(size[three], size[two], many) for _, _, many, two, three in pieces]
    scr["start"] = [vm(n) for n in (ny, nz, ny)]
    scr["ends"] = [vm(n) for n in (ny, nz, ny)]
    scr["er"] = [vm(n - 1) for n in (ny, nz, ny)]
    scr["xmid"] = [vm(zh_n), vm(zh_n), vm(ny)]
    scr["xr"] = []
    for p in range(HEADS):
        first, second = (ny, zh_n) if p < 2 else (zh_n, ny)
        scr["xr"].append([vm(first - 1, second), vm(second - 1)])
    scr["gr"] = [
        [vm(size[three] - 1, size[two], many), vm(size[two] - 1, many)]
        for _, _, many, two, three in pieces
    ]
    scr["gmid"] = [vm(size[two], many) for _, _, many, two, three in pieces]
    return scr


def local(
    geom,
    node_cache,
    node_hidden,
    node_slot,
    parent,
    child_query,
    child_kv,
    routes,
    gate_w,
    w_gate,
    w_up,
    w_down,
):
    features = w_gate.shape[1]
    vmem = pl.BlockSpec(memory_space=pltpu.VMEM)
    hbm = pl.BlockSpec(memory_space=pl.ANY)
    operands = [
        node_slot,
        routes.transpose(0, 2, 1),
        gate_w.transpose(0, 2, 1),
        parent.reshape(1, -1),
        child_query.transpose(0, 2, 1, 3),
        child_kv,
        node_hidden,
    ]
    held = [pltpu.SMEM(v.shape, v.dtype) for v in operands[:3]]
    held += [pltpu.VMEM(v.shape, v.dtype) for v in operands[3:]]
    return pl.pallas_call(
        functools.partial(kernel, geom),
        out_shape=jax.ShapeDtypeStruct(child_query.shape[:2] + (HEADS * LANES,), BF),
        in_specs=[hbm] * (len(operands) + 4),
        out_specs=vmem,
        scratch_shapes=[scratch_of(geom, features, held)],
        compiler_params=pltpu.CompilerParams(
            collective_id=0, has_side_effects=True, vmem_limit_bytes=58 * 1024 * 1024
        ),
    )(
        *operands,
        node_cache,
        w_gate,
        w_up,
        w_down,
    )


def solution(mesh):
    leaves, experts, mp = mesh.shape["leaf"], mesh.shape["expert"], mesh.shape["mp"]
    geom = (experts // 2, NY, leaves // NY, mp)
    in_specs = (
        P("leaf", "expert", None, None, None),
        P("leaf", ("expert", "mp")),
        P(),
        P(),
        P("leaf", None, ("expert", "mp"), None),
        P("leaf", "expert", None, None, None),
        P("leaf", None, None),
        P("leaf", None, None),
        P("expert", None, ("leaf", "mp")),
        P("expert", None, ("leaf", "mp")),
        P("expert", ("leaf", "mp"), None),
    )
    out_specs = P("leaf", None, ("expert", "mp"))
    return jax.shard_map(
        functools.partial(local, geom),
        mesh=mesh,
        in_specs=in_specs,
        out_specs=out_specs,
        check_vma=False,
    )
```

```python
import functools
import itertools

import jax
import jax.numpy as jnp
from jax import lax
from jax.experimental import pallas as pl
from jax.experimental.pallas import tpu as pltpu
from jax.sharding import PartitionSpec as P

F32 = jnp.float32
BF = jnp.bfloat16
SENDS = 44
RECVS = 62
LANES = 128
TOK = 8
HEADS = 3
NY = 8


class Ring:
    def __init__(self, size, me, device):
        self.size = size
        self.me = me
        self.device = device

    def at(self, offset):
        return lax.rem(self.me + offset + 2 * self.size, self.size)

    def near_first(self):
        return sorted(range(1, self.size), key=lambda k: (min(k, self.size - k), k))

    def far_first(self):
        return self.near_first()[::-1]


def interleave(jobs):
    jobs = list(jobs)
    while jobs:
        alive = []
        for job in jobs:
            try:
                next(job)
                alive.append(job)
            except StopIteration:
                pass
        jobs = alive


def kernel(
    geom,
    slot_ref,
    routes_ref,
    gate_ref,
    parent_ref,
    query_ref,
    kv_ref,
    hid_ref,
    cache_ref,
    wg_ref,
    wu_ref,
    wd_ref,
    out_ref,
    scr,
):
    nx, ny, zh_n, zl_n = geom
    nz = zh_n * zl_n
    cut_y, cut_z = cuts_of(geom)
    leaves = zh_n * ny
    tokens = leaves * TOK
    width = HEADS * LANES

    leaf = lax.axis_index("leaf")
    expert = lax.axis_index("expert")
    mp = lax.axis_index("mp")
    y = lax.rem(leaf, ny)
    zh = lax.div(leaf, ny)
    x = lax.div(expert, 2)
    core = lax.rem(expert, 2)
    z = zh * zl_n + mp

    def dev_x(k):
        return {"leaf": leaf, "expert": k * 2 + core, "mp": mp}

    def dev_y(k):
        return {"leaf": zh * ny + k, "expert": expert, "mp": mp}

    def dev_zh(k):
        return {"leaf": k * ny + y, "expert": expert, "mp": mp}

    def dev_z(k):
        return {
            "leaf": lax.div(k, zl_n) * ny + y,
            "expert": expert,
            "mp": lax.rem(k, zl_n),
        }

    sibling = {"leaf": leaf, "expert": x * 2 + (1 - core), "mp": mp}
    rx = Ring(nx, x, dev_x)
    ry = Ring(ny, y, dev_y)
    rz = Ring(nz, z, dev_z)
    rzh = Ring(zh_n, zh, dev_zh)

    send_sems, recv_sems, load_sems = scr["send"], scr["recv"], scr["load"]
    next_send = itertools.count()
    next_recv = itertools.count()
    pending = []

    def transfer(src, dst, device, send, recv):
        return pltpu.make_async_remote_copy(
            src_ref=src,
            dst_ref=dst,
            send_sem=send_sems.at[send],
            recv_sem=recv_sems.at[recv],
            device_id=device,
            device_id_type=pl.DeviceIdType.MESH,
        )

    def arrive(ref, recv):
        transfer(ref, ref, sibling, 0, recv).wait_recv()

    def gather(buf, ring, got=None):
        others = buf.at[pl.ds(0, ring.size - 1)]
        send = next(next_send)
        recvs = {k: next(next_recv) for k in range(1, ring.size if got else 2)}
        for k in ring.far_first():
            mine = buf.at[ring.me]
            transfer(mine, mine, ring.device(ring.at(k)), send, recvs[k if got else 1]).start()
        pending.append((others, send))
        yield
        if got is None:
            arrive(others, recvs[1])
        else:
            for k in ring.near_first():
                index = ring.at(-k)
                arrive(buf.at[index], recvs[k])
                got(index)

    def scatter(h, r, ring, finish):
        send, recv = next(next_send), next(next_recv)
        for k in ring.far_first():
            to = ring.at(k)
            transfer(h.at[to], r.at[k - 1], ring.device(to), send, recv).start()
        pending.append((r, send))
        yield
        arrive(r, recv)
        total = h[ring.me].astype(F32)
        for k in range(ring.size - 1):
            total = total + r[k].astype(F32)
        finish(total)

    inputs = [slot_ref, routes_ref, gate_ref, parent_ref, query_ref, kv_ref, hid_ref]
    held = scr["held"]
    small = [
        pltpu.make_async_copy(src, dst, scr["small"].at[i])
        for i, (src, dst) in enumerate(zip(inputs, held))
    ]
    for c in small:
        c.start()

    barrier = pltpu.get_barrier_semaphore()
    partners = [sibling]
    for ring in (rx, ry, rz):
        partners += [ring.device(ring.at(k)) for k in range(1, ring.size)]
    for partner in partners:
        pl.semaphore_signal(barrier, inc=1, device_id=partner, device_id_type=pl.DeviceIdType.MESH)

    loads = [
        pltpu.make_async_copy(wg_ref.at[0], scr["wgu"].at[:, pl.ds(0, LANES)], load_sems.at[0]),
        pltpu.make_async_copy(wu_ref.at[0], scr["wgu"].at[:, pl.ds(LANES, LANES)], load_sems.at[1]),
        pltpu.make_async_copy(cache_ref.at[0, 0], scr["cache"], load_sems.at[2]),
    ]
    span = zl_n * width

    def down_block(i, which):
        off = pl.multiple_of((i * 2 + which) * span, LANES)
        return wd_ref.at[0, :, pl.ds(off, span)]

    loads += [
        pltpu.make_async_copy(
            down_block(i, core),
            scr["wd"].at[pl.ds(0, LANES), pl.ds(i * span, span)],
            load_sems.at[3 + i],
        )
        for i in range(nx)
    ]
    for c in loads:
        c.start()

    for c in small:
        c.wait()
    slot_ref, routes_ref, gate_ref, parent_ref, query_ref, kv_ref, hid_ref = held
    abuf, bbuf = scr["abuf"], scr["bbuf"]
    row = lax.broadcasted_iota(jnp.int32, (TOK, LANES), 0)
    lane = lax.broadcasted_iota(jnp.int32, (TOK, LANES), 1)
    weight = jnp.zeros((TOK, LANES), F32)
    for t in range(TOK):
        w = jnp.float32(0.0)
        for k in range(2):
            w += jnp.where(
                routes_ref[t // 4, k, t % 4] == expert, gate_ref[t // 4, k, t % 4], 0.0
            )
        weight = jnp.where(row == t, w, weight)
    high = weight.astype(BF).astype(F32)
    for h in range(HEADS):
        abuf[y, zh, pl.ds(h * TOK, TOK)] = (
            query_ref[:, h].astype(F32).reshape(TOK, LANES).astype(BF)
        )
    bbuf[zh, y, pl.ds(2 * TOK, TOK)] = jnp.where(
        lane == 0, high, jnp.where(lane == 1, weight - high, 0.0)
    ).astype(BF)
    for k in range(2):
        part = kv_ref[:, 0, k].astype(F32).reshape(TOK, LANES)
        bbuf[zh, y, pl.ds(k * TOK, TOK)] = part.astype(BF)

    pl.semaphore_wait(barrier, len(partners))

    other = scr["wd"].at[pl.ds(LANES, LANES)]
    wd_send, wd_recv = next(next_send), next(next_recv)
    for i in range(nx):
        transfer(
            down_block(i, 1 - core), other.at[:, pl.ds(i * span, span)], sibling, wd_send, wd_recv
        ).start()
    pending.append((other, wd_send))

    def gather_a():
        yield from gather(abuf.at[y], rzh)
        yield from gather(abuf, ry)

    def gather_b():
        yield from gather(bbuf.at[zh], ry)
        yield from gather(bbuf, rzh)

    interleave([gather_a(), gather_b()])

    def rows_a(k):
        return jnp.concatenate(
            [
                abuf[:, i, pl.ds(k * TOK, TOK)].astype(F32).reshape(ny * TOK, LANES)
                for i in range(zh_n)
            ],
            axis=0,
        )

    def rows_b(k):
        return bbuf[:, :, pl.ds(k * TOK, TOK)].astype(F32).reshape(tokens, LANES)

    new_k = rows_b(0).astype(BF)
    new_v = rows_b(1).astype(BF)
    loads[2].wait()
    old_k = scr["cache"][0]
    old_v = scr["cache"][1]
    contract = (((1,), (1,)), ((), ()))
    row_id = lax.broadcasted_iota(jnp.int32, (tokens, tokens), 0)
    col_id = lax.broadcasted_iota(jnp.int32, (tokens, tokens), 1)
    allowed = (row_id // 4 == col_id // 4) & (col_id <= row_id)
    scale = 1.0 / LANES**0.5
    node = jnp.int32(0)
    for k in range(leaves):
        node += jnp.where(slot_ref[k] == leaf, k, 0)
    children = leaves * 2
    token_child = lax.broadcasted_iota(jnp.int32, (tokens, children), 0) // 4
    child_id = lax.broadcasted_iota(jnp.int32, (tokens, children), 1)
    here_row = (token_child == child_id) & (parent_ref[...] == node)
    mine = jnp.sum(jnp.where(here_row, 1.0, 0.0), axis=1, keepdims=True)
    xp = [scr["xp0"], scr["xp1"], scr["xp2"]]
    for p in range(HEADS):
        q = rows_a(p).astype(BF)
        s_old = lax.dot_general(q, old_k, contract, preferred_element_type=F32) * scale
        s_new = lax.dot_general(q, new_k, contract, preferred_element_type=F32) * scale
        s_new = jnp.where(allowed, s_new, -1e30)
        top = jnp.maximum(
            jnp.max(s_old, axis=1, keepdims=True), jnp.max(s_new, axis=1, keepdims=True)
        )
        e_old = jnp.exp(s_old - top)
        e_new = jnp.exp(s_new - top)
        total = jnp.sum(e_old, axis=1, keepdims=True) + jnp.sum(e_new, axis=1, keepdims=True)
        inv = 1.0 / total
        attn = jnp.dot((e_old * inv).astype(BF), old_v, preferred_element_type=F32)
        attn += jnp.dot((e_new * inv).astype(BF), new_v, preferred_element_type=F32)
        row = hid_ref[:, pl.ds(p * LANES, LANES)].astype(F32)
        here = jnp.where(mine > 0.5, attn + row, 0.0)
        here = here.reshape(zh_n, ny, TOK, LANES)
        if p < 2:
            for i in range(zh_n):
                xp[p][:, i] = here[i].astype(BF)
        else:
            xp[p][...] = here.astype(BF)

    own = scr["own"]
    start = scr["start"]
    xr = scr["xr"]
    mids = scr["xmid"]
    xs = scr["xs"]
    firsts = (ry, rz, ry)

    def home(p):
        first, second = (ry, rzh) if p < 2 else (rzh, ry)

        def keep(v):
            mids[p][...] = v.astype(BF)

        yield from scatter(xp[p], xr[p][0], first, keep)

        def final(v):
            w = v.astype(BF)
            xs[p] = w
            start[p][firsts[p].me] = w

        yield from scatter(mids[p], xr[p][1], second, final)
        yield from gather(start[p], firsts[p])

    homes = [home(p) for p in range(HEADS)]
    for _ in range(3):
        for job in homes:
            next(job)

    sib = scr["sib"]
    d2d = []
    rings = {"x": rx, "y": ry, "z": rz}
    pieces = pieces_of(geom)

    def everywhere(k):
        p, low, many, two, three = pieces[k]
        two, three = rings[two], rings[three]
        own[k][three.me, two.me] = start[p][pl.ds(low, many)]
        yield from gather(own[k].at[three.me], two)

        send, recv = next(next_send), next(next_recv)

        def forward(index):
            transfer(own[k].at[index], sib[k].at[index], sibling, send, recv).start()

        pending.append((own[k], send))
        d2d.append((sib[k], recv))
        forward(three.me)
        yield from gather(own[k], three, forward)

    spread = [everywhere(k) for k in range(len(pieces))]
    for p in range(HEADS):
        interleave([homes[p]])
        for k in (0, 1, 2, 3, 4):
            if pieces[k][0] == p:
                next(spread[k])
    interleave([spread[k] for k in (0, 2, 1, 3, 4)])

    def tiles(refs, p, xi, m, i):
        zi = i * zl_n + m
        if p == 0:
            return [(refs[0].at[zi, xi], 0, cut_y), (refs[1].at[xi, zi], cut_y, ny - cut_y)]
        if p == 1:
            if i * zl_n < cut_z:
                return [(refs[2].at[:, xi, zi], 0, ny)]
            return [(refs[3].at[xi, :, zi - cut_z], 0, ny)]
        return [(refs[4].at[xi, zi], 0, ny)]

    def rows_of(refs, p, xi, m, i):
        parts = [ref[...].astype(F32) for ref, _, _ in tiles(refs, p, xi, m, i)]
        part = parts[0] if len(parts) == 1 else jnp.concatenate(parts, axis=0)
        return part.reshape(ny * TOK, LANES)

    acc = scr["acc"]
    acc[...] = jnp.zeros_like(acc)
    for c in loads[:2] + loads[3:]:
        c.wait()
    blocks = nx * zl_n

    def up(refs, which):
        @pl.loop(0, blocks)
        def _(j):
            xi, m = lax.div(j, zl_n), lax.rem(j, zl_n)
            cols = []
            for p in range(HEADS):
                cols.append(
                    jnp.concatenate(
                        [rows_of(refs, p, xi, m, i) for i in range(zh_n)],
                        axis=0,
                    ).astype(BF)
                )
            rows = jnp.concatenate(cols, axis=1)
            off = pl.multiple_of(((xi * 2 + which) * zl_n + m) * width, LANES)
            acc[...] += jnp.dot(rows, scr["wgu"][pl.ds(off, width), :], preferred_element_type=F32)

    up(own, core)
    for ref, recv in d2d:
        arrive(ref, recv)
    up(sib, 1 - core)

    gates = rows_b(2)
    gate = gates[:, 0:1] + gates[:, 1:2]
    g = acc[:, pl.ds(0, LANES)]
    u = acc[:, pl.ds(LANES, LANES)]
    units = (g * (1.0 / (1.0 + jnp.exp(-g))) * u).astype(BF).astype(F32)
    mine_units, other_units = scr["units"], scr["units_other"]
    mine_units[...] = (units * gate).astype(BF)
    u_send, u_recv = next(next_send), next(next_recv)
    transfer(mine_units, other_units, sibling, u_send, u_recv).start()
    pending.append((other_units, u_send))
    ho = scr["ho"]
    arrive(other, wd_recv)
    arrive(other_units, u_recv)

    def down(parts):
        count = len(parts) * LANES

        @pl.loop(0, blocks)
        def _(j):
            xi, m = lax.div(j, zl_n), lax.rem(j, zl_n)
            both = jnp.concatenate([mine_units[...], other_units[...]], axis=1)
            off = pl.multiple_of(j * width + parts[0] * LANES, LANES)
            o = jnp.dot(both, scr["wd"][:, pl.ds(off, count)], preferred_element_type=F32)
            for k, p in enumerate(parts):
                part = o[:, k * LANES : (k + 1) * LANES].reshape(zh_n, ny, TOK, LANES)
                for i in range(zh_n):
                    for ref, low, many in tiles(ho, p, xi, m, i):
                        ref[...] = part[i][low : low + many].astype(BF)

    gr, gmid, ends, er = scr["gr"], scr["gmid"], scr["ends"], scr["er"]

    def back(k):
        p, low, many, two, three = pieces[k]
        if k == 0:
            down((0, 1))
        if p == 2:
            down((2,))

        def keep(v):
            gmid[k][...] = v.astype(BF)

        def end(v):
            ends[p][pl.ds(low, many)] = v.astype(BF)

        yield from scatter(ho[k], gr[k][0], rings[three], keep)
        yield from scatter(gmid[k], gr[k][1], rings[two], end)

    def last(p):
        def final(v):
            w = (xs[p].astype(F32) + v).astype(BF)
            for c in range(2):
                out_ref[c, :, pl.ds(p * LANES, LANES)] = w[c * 4 : c * 4 + 4]

        yield from scatter(ends[p], er[p], firsts[p], final)

    backs = [back(k) for k in range(len(pieces))]
    lasts = [last(p) for p in range(HEADS)]
    for k in (0, 2, 1, 3, 4):
        next(backs[k])
    for k in (1, 3, 4, 0, 2):
        next(backs[k])
    for k in (1, 3, 4, 0, 2):
        interleave([backs[k]])
        if k in (4, 0, 2):
            next(lasts[pieces[k][0]])
    interleave([lasts[p] for p in (2, 0, 1)])

    for ref, send in pending:
        transfer(ref, ref, sibling, send, 0).wait_send()


def cuts_of(geom):
    nx, ny, zh_n, zl_n = geom
    return ny * 3 // 4, zh_n * 3 // 4 * zl_n


def pieces_of(geom):
    nx, ny, zh_n, zl_n = geom
    nz = zh_n * zl_n
    cut_y, cut_z = cuts_of(geom)
    return [
        (0, 0, cut_y, "x", "z"),
        (0, cut_y, ny - cut_y, "z", "x"),
        (1, 0, cut_z, "x", "y"),
        (1, cut_z, nz - cut_z, "y", "x"),
        (2, 0, ny, "z", "x"),
    ]


def scratch_of(geom, features, held):
    nx, ny, zh_n, zl_n = geom
    nz = zh_n * zl_n
    tokens = zh_n * ny * TOK
    tile = (TOK, LANES)
    vm = lambda *shape: pltpu.VMEM(shape + tile, BF)
    size = {"x": nx, "y": ny, "z": nz}
    pieces = pieces_of(geom)
    scr = {
        "send": pltpu.SemaphoreType.DMA((SENDS,)),
        "recv": pltpu.SemaphoreType.DMA((RECVS,)),
        "held": held,
        "small": pltpu.SemaphoreType.DMA((len(held),)),
        "load": pltpu.SemaphoreType.DMA((3 + nx,)),
        "cache": pltpu.VMEM((2, 256, LANES), BF),
        "wgu": pltpu.VMEM((features, 2 * LANES), BF),
        "wd": pltpu.VMEM((2 * LANES, features // 2), BF),
        "abuf": pltpu.VMEM((ny, zh_n, HEADS * TOK, LANES), BF),
        "bbuf": pltpu.VMEM((zh_n, ny, 3 * TOK, LANES), BF),
        "xs": vm(HEADS),
        "acc": pltpu.VMEM((tokens, 2 * LANES), F32),
        "units": pltpu.VMEM((tokens, LANES), BF),
        "units_other": pltpu.VMEM((tokens, LANES), BF),
    }
    for p in range(HEADS):
        scr["xp" + str(p)] = vm(ny, zh_n) if p < 2 else vm(zh_n, ny)
    for name in ("own", "sib", "ho"):
        scr[name] = [vm(size[three], size[two], many) for _, _, many, two, three in pieces]
    scr["start"] = [vm(n) for n in (ny, nz, ny)]
    scr["ends"] = [vm(n) for n in (ny, nz, ny)]
    scr["er"] = [vm(n - 1) for n in (ny, nz, ny)]
    scr["xmid"] = [vm(zh_n), vm(zh_n), vm(ny)]
    scr["xr"] = []
    for p in range(HEADS):
        first, second = (ny, zh_n) if p < 2 else (zh_n, ny)
        scr["xr"].append([vm(first - 1, second), vm(second - 1)])
    scr["gr"] = [
        [vm(size[three] - 1, size[two], many), vm(size[two] - 1, many)]
        for _, _, many, two, three in pieces
    ]
    scr["gmid"] = [vm(size[two], many) for _, _, many, two, three in pieces]
    return scr


def local(
    geom,
    node_cache,
    node_hidden,
    node_slot,
    parent,
    child_query,
    child_kv,
    routes,
    gate_w,
    w_gate,
    w_up,
    w_down,
):
    features = w_gate.shape[1]
    vmem = pl.BlockSpec(memory_space=pltpu.VMEM)
    hbm = pl.BlockSpec(memory_space=pl.ANY)
    operands = [
        node_slot,
        routes.transpose(0, 2, 1),
        gate_w.transpose(0, 2, 1),
        parent.reshape(1, -1),
        child_query.transpose(0, 2, 1, 3),
        child_kv,
        node_hidden,
    ]
    held = [pltpu.SMEM(v.shape, v.dtype) for v in operands[:3]]
    held += [pltpu.VMEM(v.shape, v.dtype) for v in operands[3:]]
    return pl.pallas_call(
        functools.partial(kernel, geom),
        out_shape=jax.ShapeDtypeStruct(child_query.shape[:2] + (HEADS * LANES,), BF),
        in_specs=[hbm] * (len(operands) + 4),
        out_specs=vmem,
        scratch_shapes=[scratch_of(geom, features, held)],
        compiler_params=pltpu.CompilerParams(
            collective_id=0, has_side_effects=True, vmem_limit_bytes=58 * 1024 * 1024
        ),
    )(
        *operands,
        node_cache,
        w_gate,
        w_up,
        w_down,
    )


def solution(mesh):
    leaves, experts, mp = mesh.shape["leaf"], mesh.shape["expert"], mesh.shape["mp"]
    geom = (experts // 2, NY, leaves // NY, mp)
    in_specs = (
        P("leaf", "expert", None, None, None),
        P("leaf", ("expert", "mp")),
        P(),
        P(),
        P("leaf", None, ("expert", "mp"), None),
        P("leaf", "expert", None, None, None),
        P("leaf", None, None),
        P("leaf", None, None),
        P("expert", None, ("leaf", "mp")),
        P("expert", None, ("leaf", "mp")),
        P("expert", ("leaf", "mp"), None),
    )
    out_specs = P("leaf", None, ("expert", "mp"))
    return jax.shard_map(
        functools.partial(local, geom),
        mesh=mesh,
        in_specs=in_specs,
        out_specs=out_specs,
        check_vma=False,
    )
```

```python
import functools
import itertools

import jax
import jax.numpy as jnp
from jax import lax
from jax.experimental import pallas as pl
from jax.experimental.pallas import tpu as pltpu
from jax.sharding import PartitionSpec as P

F32 = jnp.float32
BF = jnp.bfloat16
SENDS = 44
RECVS = 62
LANES = 128
TOK = 8
HEADS = 3
NY = 8


class Ring:
    def __init__(self, size, me, device):
        self.size = size
        self.me = me
        self.device = device

    def at(self, offset):
        return lax.rem(self.me + offset + 2 * self.size, self.size)

    def near_first(self):
        return sorted(range(1, self.size), key=lambda k: (min(k, self.size - k), k))

    def far_first(self):
        return self.near_first()[::-1]


def interleave(jobs):
    jobs = list(jobs)
    while jobs:
        alive = []
        for job in jobs:
            try:
                next(job)
                alive.append(job)
            except StopIteration:
                pass
        jobs = alive


def kernel(
    geom,
    slot_ref,
    routes_ref,
    gate_ref,
    parent_ref,
    query_ref,
    kv_ref,
    hid_ref,
    cache_ref,
    wg_ref,
    wu_ref,
    wd_ref,
    out_ref,
    scr,
):
    nx, ny, zh_n, zl_n = geom
    nz = zh_n * zl_n
    cut_y, cut_z = cuts_of(geom)
    leaves = zh_n * ny
    tokens = leaves * TOK
    width = HEADS * LANES

    leaf = lax.axis_index("leaf")
    expert = lax.axis_index("expert")
    mp = lax.axis_index("mp")
    y = lax.rem(leaf, ny)
    zh = lax.div(leaf, ny)
    x = lax.div(expert, 2)
    core = lax.rem(expert, 2)
    z = zh * zl_n + mp

    def dev_x(k):
        return {"leaf": leaf, "expert": k * 2 + core, "mp": mp}

    def dev_y(k):
        return {"leaf": zh * ny + k, "expert": expert, "mp": mp}

    def dev_zh(k):
        return {"leaf": k * ny + y, "expert": expert, "mp": mp}

    def dev_z(k):
        return {
            "leaf": lax.div(k, zl_n) * ny + y,
            "expert": expert,
            "mp": lax.rem(k, zl_n),
        }

    sibling = {"leaf": leaf, "expert": x * 2 + (1 - core), "mp": mp}
    rx = Ring(nx, x, dev_x)
    ry = Ring(ny, y, dev_y)
    rz = Ring(nz, z, dev_z)
    rzh = Ring(zh_n, zh, dev_zh)

    send_sems, recv_sems, load_sems = scr["send"], scr["recv"], scr["load"]
    next_send = itertools.count()
    next_recv = itertools.count()
    pending = []

    def transfer(src, dst, device, send, recv):
        return pltpu.make_async_remote_copy(
            src_ref=src,
            dst_ref=dst,
            send_sem=send_sems.at[send],
            recv_sem=recv_sems.at[recv],
            device_id=device,
            device_id_type=pl.DeviceIdType.MESH,
        )

    def arrive(ref, recv):
        transfer(ref, ref, sibling, 0, recv).wait_recv()

    def gather(buf, ring, got=None):
        others = buf.at[pl.ds(0, ring.size - 1)]
        send = next(next_send)
        recvs = {k: next(next_recv) for k in range(1, ring.size if got else 2)}
        for k in ring.far_first():
            mine = buf.at[ring.me]
            transfer(mine, mine, ring.device(ring.at(k)), send, recvs[k if got else 1]).start()
        pending.append((others, send))
        yield
        if got is None:
            arrive(others, recvs[1])
        else:
            for k in ring.near_first():
                index = ring.at(-k)
                arrive(buf.at[index], recvs[k])
                got(index)
                yield

    def scatter(h, r, ring, finish):
        send, recv = next(next_send), next(next_recv)
        for k in ring.far_first():
            to = ring.at(k)
            transfer(h.at[to], r.at[k - 1], ring.device(to), send, recv).start()
        pending.append((r, send))
        yield
        arrive(r, recv)
        total = h[ring.me].astype(F32)
        for k in range(ring.size - 1):
            total = total + r[k].astype(F32)
        finish(total)

    barrier = pltpu.get_barrier_semaphore()
    far = [
        (min(k, ring.size - k), ring.device(ring.at(k)))
        for ring in (rz, ry, rx)
        for k in range(1, ring.size)
    ]
    partners = [device for _, device in sorted(far, key=lambda entry: -entry[0])] + [sibling]
    for partner in partners:
        pl.semaphore_signal(barrier, inc=1, device_id=partner, device_id_type=pl.DeviceIdType.MESH)

    inputs = [slot_ref, routes_ref, gate_ref, parent_ref, query_ref, kv_ref, hid_ref]
    held = scr["held"]
    small = [
        pltpu.make_async_copy(src, dst, scr["small"].at[i])
        for i, (src, dst) in enumerate(zip(inputs, held))
    ]
    for c in small:
        c.start()

    loads = [
        pltpu.make_async_copy(wg_ref.at[0], scr["wgu"].at[:, pl.ds(0, LANES)], load_sems.at[0]),
        pltpu.make_async_copy(wu_ref.at[0], scr["wgu"].at[:, pl.ds(LANES, LANES)], load_sems.at[1]),
        pltpu.make_async_copy(cache_ref.at[0, 0], scr["cache"], load_sems.at[2]),
    ]
    span = zl_n * width

    def down_block(i, which):
        off = pl.multiple_of((i * 2 + which) * span, LANES)
        return wd_ref.at[0, :, pl.ds(off, span)]

    loads += [
        pltpu.make_async_copy(
            down_block(i, core),
            scr["wd"].at[pl.ds(0, LANES), pl.ds(i * span, span)],
            load_sems.at[3 + i],
        )
        for i in range(nx)
    ]
    for c in loads:
        c.start()

    for c in small:
        c.wait()
    slot_ref, routes_ref, gate_ref, parent_ref, query_ref, kv_ref, hid_ref = held
    abuf, bbuf = scr["abuf"], scr["bbuf"]
    row = lax.broadcasted_iota(jnp.int32, (TOK, LANES), 0)
    lane = lax.broadcasted_iota(jnp.int32, (TOK, LANES), 1)
    weight = jnp.zeros((TOK, LANES), F32)
    for t in range(TOK):
        w = jnp.float32(0.0)
        for k in range(2):
            w += jnp.where(
                routes_ref[t // 4, k, t % 4] == expert, gate_ref[t // 4, k, t % 4], 0.0
            )
        weight = jnp.where(row == t, w, weight)
    high = weight.astype(BF).astype(F32)
    for h in range(HEADS):
        abuf[y, zh, pl.ds(h * TOK, TOK)] = (
            query_ref[:, h].astype(F32).reshape(TOK, LANES).astype(BF)
        )
    bbuf[zh, y, pl.ds(2 * TOK, TOK)] = jnp.where(
        lane == 0, high, jnp.where(lane == 1, weight - high, 0.0)
    ).astype(BF)
    for k in range(2):
        part = kv_ref[:, 0, k].astype(F32).reshape(TOK, LANES)
        bbuf[zh, y, pl.ds(k * TOK, TOK)] = part.astype(BF)

    pl.semaphore_wait(barrier, len(partners))

    other = scr["wd"].at[pl.ds(LANES, LANES)]
    wd_send, wd_recv = next(next_send), next(next_recv)
    for i in range(nx):
        transfer(
            down_block(i, 1 - core), other.at[:, pl.ds(i * span, span)], sibling, wd_send, wd_recv
        ).start()
    pending.append((other, wd_send))

    def gather_a():
        yield from gather(abuf.at[y], rzh)
        yield from gather(abuf, ry)

    def gather_b():
        yield from gather(bbuf.at[zh], ry)
        yield from gather(bbuf, rzh)

    interleave([gather_a(), gather_b()])

    def rows_a(k):
        return jnp.concatenate(
            [
                abuf[:, i, pl.ds(k * TOK, TOK)].astype(F32).reshape(ny * TOK, LANES)
                for i in range(zh_n)
            ],
            axis=0,
        )

    def rows_b(k):
        return bbuf[:, :, pl.ds(k * TOK, TOK)].astype(F32).reshape(tokens, LANES)

    new_k = rows_b(0).astype(BF)
    new_v = rows_b(1).astype(BF)
    loads[2].wait()
    old_k = scr["cache"][0]
    old_v = scr["cache"][1]
    contract = (((1,), (1,)), ((), ()))
    row_id = lax.broadcasted_iota(jnp.int32, (tokens, tokens), 0)
    col_id = lax.broadcasted_iota(jnp.int32, (tokens, tokens), 1)
    allowed = (row_id // 4 == col_id // 4) & (col_id <= row_id)
    scale = 1.0 / LANES**0.5
    node = jnp.int32(0)
    for k in range(leaves):
        node += jnp.where(slot_ref[k] == leaf, k, 0)
    children = leaves * 2
    token_child = lax.broadcasted_iota(jnp.int32, (tokens, children), 0) // 4
    child_id = lax.broadcasted_iota(jnp.int32, (tokens, children), 1)
    here_row = (token_child == child_id) & (parent_ref[...] == node)
    mine = jnp.sum(jnp.where(here_row, 1.0, 0.0), axis=1, keepdims=True)
    xp = [scr["xp0"], scr["xp1"], scr["xp2"]]
    own = scr["own"]
    start = scr["start"]
    xr = scr["xr"]
    mids = scr["xmid"]
    xs = scr["xs"]
    firsts = (ry, rz, ry)

    def home(p):
        first, second = (ry, rzh) if p < 2 else (rzh, ry)

        def keep(v):
            mids[p][...] = v.astype(BF)

        yield from scatter(xp[p], xr[p][0], first, keep)

        def final(v):
            w = v.astype(BF)
            xs[p] = w
            start[p][firsts[p].me] = w

        yield from scatter(mids[p], xr[p][1], second, final)
        yield from gather(start[p], firsts[p])

    homes = [home(p) for p in range(HEADS)]
    for p in range(HEADS):
        q = rows_a(p).astype(BF)
        s_old = lax.dot_general(q, old_k, contract, preferred_element_type=F32) * scale
        s_new = lax.dot_general(q, new_k, contract, preferred_element_type=F32) * scale
        s_new = jnp.where(allowed, s_new, -1e30)
        top = jnp.maximum(
            jnp.max(s_old, axis=1, keepdims=True), jnp.max(s_new, axis=1, keepdims=True)
        )
        e_old = jnp.exp(s_old - top)
        e_new = jnp.exp(s_new - top)
        total = jnp.sum(e_old, axis=1, keepdims=True) + jnp.sum(e_new, axis=1, keepdims=True)
        inv = 1.0 / total
        attn = jnp.dot((e_old * inv).astype(BF), old_v, preferred_element_type=F32)
        attn += jnp.dot((e_new * inv).astype(BF), new_v, preferred_element_type=F32)
        row = hid_ref[:, pl.ds(p * LANES, LANES)].astype(F32)
        here = jnp.where(mine > 0.5, attn + row, 0.0)
        here = here.reshape(zh_n, ny, TOK, LANES)
        if p < 2:
            for i in range(zh_n):
                xp[p][:, i] = here[i].astype(BF)
        else:
            xp[p][...] = here.astype(BF)
        next(homes[p])

    for _ in range(2):
        for job in homes:
            next(job)

    sib = scr["sib"]
    d2d = []
    rings = {"x": rx, "y": ry, "z": rz}
    pieces = pieces_of(geom)

    def everywhere(k):
        p, low, many, two, three = pieces[k]
        two, three = rings[two], rings[three]
        own[k][three.me, two.me] = start[p][pl.ds(low, many)]
        yield from gather(own[k].at[three.me], two)

        send, recv = next(next_send), next(next_recv)

        def forward(index):
            transfer(own[k].at[index], sib[k].at[index], sibling, send, recv).start()

        pending.append((own[k], send))
        d2d.append((sib[k], recv))
        forward(three.me)
        yield from gather(own[k], three, forward)

    spread = [everywhere(k) for k in range(len(pieces))]
    for p in range(HEADS):
        interleave([homes[p]])
        for k in (0, 1, 2, 3, 4):
            if pieces[k][0] == p:
                next(spread[k])
    interleave([spread[k] for k in (0, 2, 1, 3, 4)])

    def tiles(refs, p, xi, m, i):
        zi = i * zl_n + m
        if p == 0:
            return [(refs[0].at[zi, xi], 0, cut_y), (refs[1].at[xi, zi], cut_y, ny - cut_y)]
        if p == 1:
            if i * zl_n < cut_z:
                return [(refs[2].at[:, xi, zi], 0, ny)]
            return [(refs[3].at[xi, :, zi - cut_z], 0, ny)]
        return [(refs[4].at[xi, zi], 0, ny)]

    def rows_of(refs, p, xi, m, i):
        parts = [ref[...].astype(F32) for ref, _, _ in tiles(refs, p, xi, m, i)]
        part = parts[0] if len(parts) == 1 else jnp.concatenate(parts, axis=0)
        return part.reshape(ny * TOK, LANES)

    acc = scr["acc"]
    acc[...] = jnp.zeros_like(acc)
    for c in loads[:2] + loads[3:]:
        c.wait()
    blocks = nx * zl_n

    def up(refs, which):
        @pl.loop(0, blocks)
        def _(j):
            xi, m = lax.div(j, zl_n), lax.rem(j, zl_n)
            cols = []
            for p in range(HEADS):
                cols.append(
                    jnp.concatenate(
                        [rows_of(refs, p, xi, m, i) for i in range(zh_n)],
                        axis=0,
                    ).astype(BF)
                )
            rows = jnp.concatenate(cols, axis=1)
            off = pl.multiple_of(((xi * 2 + which) * zl_n + m) * width, LANES)
            acc[...] += jnp.dot(rows, scr["wgu"][pl.ds(off, width), :], preferred_element_type=F32)

    up(own, core)
    for ref, recv in d2d:
        arrive(ref, recv)
    up(sib, 1 - core)

    gates = rows_b(2)
    gate = gates[:, 0:1] + gates[:, 1:2]
    g = acc[:, pl.ds(0, LANES)]
    u = acc[:, pl.ds(LANES, LANES)]
    units = (g * (1.0 / (1.0 + jnp.exp(-g))) * u).astype(BF).astype(F32)
    mine_units, other_units = scr["units"], scr["units_other"]
    mine_units[...] = (units * gate).astype(BF)
    u_send, u_recv = next(next_send), next(next_recv)
    transfer(mine_units, other_units, sibling, u_send, u_recv).start()
    pending.append((other_units, u_send))
    ho = scr["ho"]
    arrive(other, wd_recv)
    arrive(other_units, u_recv)

    def down(parts):
        count = len(parts) * LANES

        @pl.loop(0, blocks)
        def _(j):
            xi, m = lax.div(j, zl_n), lax.rem(j, zl_n)
            both = jnp.concatenate([mine_units[...], other_units[...]], axis=1)
            off = pl.multiple_of(j * width + parts[0] * LANES, LANES)
            o = jnp.dot(both, scr["wd"][:, pl.ds(off, count)], preferred_element_type=F32)
            for k, p in enumerate(parts):
                part = o[:, k * LANES : (k + 1) * LANES].reshape(zh_n, ny, TOK, LANES)
                for i in range(zh_n):
                    for ref, low, many in tiles(ho, p, xi, m, i):
                        ref[...] = part[i][low : low + many].astype(BF)

    gr, gmid, ends, er = scr["gr"], scr["gmid"], scr["ends"], scr["er"]

    def back(k):
        p, low, many, two, three = pieces[k]
        if k == 0:
            down((0, 1))
        if p == 2:
            down((2,))

        def keep(v):
            gmid[k][...] = v.astype(BF)

        def end(v):
            ends[p][pl.ds(low, many)] = v.astype(BF)

        yield from scatter(ho[k], gr[k][0], rings[three], keep)
        yield from scatter(gmid[k], gr[k][1], rings[two], end)

    def last(p):
        def final(v):
            w = (xs[p].astype(F32) + v).astype(BF)
            for c in range(2):
                out_ref[c, :, pl.ds(p * LANES, LANES)] = w[c * 4 : c * 4 + 4]

        yield from scatter(ends[p], er[p], firsts[p], final)

    backs = [back(k) for k in range(len(pieces))]
    lasts = [last(p) for p in range(HEADS)]
    for k in (0, 2, 1, 3, 4):
        next(backs[k])
    for k in (1, 3, 4, 0, 2):
        next(backs[k])
    for k in (1, 3, 4, 0, 2):
        interleave([backs[k]])
        if k in (4, 0, 2):
            next(lasts[pieces[k][0]])
    interleave([lasts[p] for p in (2, 0, 1)])

    for ref, send in pending:
        transfer(ref, ref, sibling, send, 0).wait_send()


def cuts_of(geom):
    nx, ny, zh_n, zl_n = geom
    return ny * 3 // 4, zh_n * 3 // 4 * zl_n


def pieces_of(geom):
    nx, ny, zh_n, zl_n = geom
    nz = zh_n * zl_n
    cut_y, cut_z = cuts_of(geom)
    return [
        (0, 0, cut_y, "x", "z"),
        (0, cut_y, ny - cut_y, "z", "x"),
        (1, 0, cut_z, "x", "y"),
        (1, cut_z, nz - cut_z, "y", "x"),
        (2, 0, ny, "z", "x"),
    ]


def scratch_of(geom, features, held):
    nx, ny, zh_n, zl_n = geom
    nz = zh_n * zl_n
    tokens = zh_n * ny * TOK
    tile = (TOK, LANES)
    vm = lambda *shape: pltpu.VMEM(shape + tile, BF)
    size = {"x": nx, "y": ny, "z": nz}
    pieces = pieces_of(geom)
    scr = {
        "send": pltpu.SemaphoreType.DMA((SENDS,)),
        "recv": pltpu.SemaphoreType.DMA((RECVS,)),
        "held": held,
        "small": pltpu.SemaphoreType.DMA((len(held),)),
        "load": pltpu.SemaphoreType.DMA((3 + nx,)),
        "cache": pltpu.VMEM((2, 256, LANES), BF),
        "wgu": pltpu.VMEM((features, 2 * LANES), BF),
        "wd": pltpu.VMEM((2 * LANES, features // 2), BF),
        "abuf": pltpu.VMEM((ny, zh_n, HEADS * TOK, LANES), BF),
        "bbuf": pltpu.VMEM((zh_n, ny, 3 * TOK, LANES), BF),
        "xs": vm(HEADS),
        "acc": pltpu.VMEM((tokens, 2 * LANES), F32),
        "units": pltpu.VMEM((tokens, LANES), BF),
        "units_other": pltpu.VMEM((tokens, LANES), BF),
    }
    for p in range(HEADS):
        scr["xp" + str(p)] = vm(ny, zh_n) if p < 2 else vm(zh_n, ny)
    for name in ("own", "sib", "ho"):
        scr[name] = [vm(size[three], size[two], many) for _, _, many, two, three in pieces]
    scr["start"] = [vm(n) for n in (ny, nz, ny)]
    scr["ends"] = [vm(n) for n in (ny, nz, ny)]
    scr["er"] = [vm(n - 1) for n in (ny, nz, ny)]
    scr["xmid"] = [vm(zh_n), vm(zh_n), vm(ny)]
    scr["xr"] = []
    for p in range(HEADS):
        first, second = (ny, zh_n) if p < 2 else (zh_n, ny)
        scr["xr"].append([vm(first - 1, second), vm(second - 1)])
    scr["gr"] = [
        [vm(size[three] - 1, size[two], many), vm(size[two] - 1, many)]
        for _, _, many, two, three in pieces
    ]
    scr["gmid"] = [vm(size[two], many) for _, _, many, two, three in pieces]
    return scr


def local(
    geom,
    node_cache,
    node_hidden,
    node_slot,
    parent,
    child_query,
    child_kv,
    routes,
    gate_w,
    w_gate,
    w_up,
    w_down,
):
    features = w_gate.shape[1]
    vmem = pl.BlockSpec(memory_space=pltpu.VMEM)
    hbm = pl.BlockSpec(memory_space=pl.ANY)
    operands = [
        node_slot,
        routes.transpose(0, 2, 1),
        gate_w.transpose(0, 2, 1),
        parent.reshape(1, -1),
        child_query.transpose(0, 2, 1, 3),
        child_kv,
        node_hidden,
    ]
    held = [pltpu.SMEM(v.shape, v.dtype) for v in operands[:3]]
    held += [pltpu.VMEM(v.shape, v.dtype) for v in operands[3:]]
    return pl.pallas_call(
        functools.partial(kernel, geom),
        out_shape=jax.ShapeDtypeStruct(child_query.shape[:2] + (HEADS * LANES,), BF),
        in_specs=[hbm] * (len(operands) + 4),
        out_specs=vmem,
        scratch_shapes=[scratch_of(geom, features, held)],
        compiler_params=pltpu.CompilerParams(
            collective_id=0, has_side_effects=True, vmem_limit_bytes=58 * 1024 * 1024
        ),
    )(
        *operands,
        node_cache,
        w_gate,
        w_up,
        w_down,
    )


def solution(mesh):
    leaves, experts, mp = mesh.shape["leaf"], mesh.shape["expert"], mesh.shape["mp"]
    geom = (experts // 2, NY, leaves // NY, mp)
    in_specs = (
        P("leaf", "expert", None, None, None),
        P("leaf", ("expert", "mp")),
        P(),
        P(),
        P("leaf", None, ("expert", "mp"), None),
        P("leaf", "expert", None, None, None),
        P("leaf", None, None),
        P("leaf", None, None),
        P("expert", None, ("leaf", "mp")),
        P("expert", None, ("leaf", "mp")),
        P("expert", ("leaf", "mp"), None),
    )
    out_specs = P("leaf", None, ("expert", "mp"))
    return jax.shard_map(
        functools.partial(local, geom),
        mesh=mesh,
        in_specs=in_specs,
        out_specs=out_specs,
        check_vma=False,
    )
```

```python
import functools
import itertools

import jax
import jax.numpy as jnp
from jax import lax
from jax.experimental import pallas as pl
from jax.experimental.pallas import tpu as pltpu
from jax.sharding import PartitionSpec as P

F32 = jnp.float32
BF = jnp.bfloat16
SENDS = 44
RECVS = 62
LANES = 128
TOK = 8
HEADS = 3
NY = 8


class Ring:
    def __init__(self, size, me, device):
        self.size = size
        self.me = me
        self.device = device

    def at(self, offset):
        return lax.rem(self.me + offset + 2 * self.size, self.size)

    def near_first(self):
        return sorted(range(1, self.size), key=lambda k: (min(k, self.size - k), k))

    def far_first(self):
        return self.near_first()[::-1]


def interleave(jobs):
    jobs = list(jobs)
    while jobs:
        alive = []
        for job in jobs:
            try:
                next(job)
                alive.append(job)
            except StopIteration:
                pass
        jobs = alive


def kernel(
    geom,
    slot_ref,
    routes_ref,
    gate_ref,
    parent_ref,
    query_ref,
    kv_ref,
    hid_ref,
    cache_ref,
    wg_ref,
    wu_ref,
    wd_ref,
    out_ref,
    scr,
):
    nx, ny, zh_n, zl_n = geom
    nz = zh_n * zl_n
    cut_y, cut_z = cuts_of(geom)
    leaves = zh_n * ny
    tokens = leaves * TOK
    width = HEADS * LANES

    leaf = lax.axis_index("leaf")
    expert = lax.axis_index("expert")
    mp = lax.axis_index("mp")
    y = lax.rem(leaf, ny)
    zh = lax.div(leaf, ny)
    x = lax.div(expert, 2)
    core = lax.rem(expert, 2)
    z = zh * zl_n + mp

    def dev_x(k):
        return {"leaf": leaf, "expert": k * 2 + core, "mp": mp}

    def dev_y(k):
        return {"leaf": zh * ny + k, "expert": expert, "mp": mp}

    def dev_zh(k):
        return {"leaf": k * ny + y, "expert": expert, "mp": mp}

    def dev_z(k):
        return {
            "leaf": lax.div(k, zl_n) * ny + y,
            "expert": expert,
            "mp": lax.rem(k, zl_n),
        }

    sibling = {"leaf": leaf, "expert": x * 2 + (1 - core), "mp": mp}
    rx = Ring(nx, x, dev_x)
    ry = Ring(ny, y, dev_y)
    rz = Ring(nz, z, dev_z)
    rzh = Ring(zh_n, zh, dev_zh)

    send_sems, recv_sems, load_sems = scr["send"], scr["recv"], scr["load"]
    next_send = itertools.count()
    next_recv = itertools.count()
    pending = []

    def transfer(src, dst, device, send, recv):
        return pltpu.make_async_remote_copy(
            src_ref=src,
            dst_ref=dst,
            send_sem=send_sems.at[send],
            recv_sem=recv_sems.at[recv],
            device_id=device,
            device_id_type=pl.DeviceIdType.MESH,
        )

    def arrive(ref, recv):
        transfer(ref, ref, sibling, 0, recv).wait_recv()

    def gather(buf, ring, got=None):
        others = buf.at[pl.ds(0, ring.size - 1)]
        send = next(next_send)
        recvs = {k: next(next_recv) for k in range(1, ring.size if got else 2)}
        for k in ring.far_first():
            mine = buf.at[ring.me]
            transfer(mine, mine, ring.device(ring.at(k)), send, recvs[k if got else 1]).start()
        pending.append((others, send))
        yield
        if got is None:
            arrive(others, recvs[1])
        else:
            for k in ring.near_first():
                index = ring.at(-k)
                arrive(buf.at[index], recvs[k])
                got(index)
                yield

    def scatter(h, r, ring, finish):
        send, recv = next(next_send), next(next_recv)
        for k in ring.far_first():
            to = ring.at(k)
            transfer(h.at[to], r.at[k - 1], ring.device(to), send, recv).start()
        pending.append((r, send))
        yield
        arrive(r, recv)
        total = h[ring.me].astype(F32)
        for k in range(ring.size - 1):
            total = total + r[k].astype(F32)
        finish(total)

    barrier = pltpu.get_barrier_semaphore()
    far = [
        (min(k, ring.size - k), ring.device(ring.at(k)))
        for ring in (rz, ry, rx)
        for k in range(1, ring.size)
    ]
    partners = [device for _, device in sorted(far, key=lambda entry: -entry[0])] + [sibling]
    for partner in partners:
        pl.semaphore_signal(barrier, inc=1, device_id=partner, device_id_type=pl.DeviceIdType.MESH)

    inputs = [slot_ref, routes_ref, gate_ref, parent_ref, query_ref, kv_ref, hid_ref]
    held = scr["held"]
    small = [
        pltpu.make_async_copy(src, dst, scr["small"].at[i])
        for i, (src, dst) in enumerate(zip(inputs, held))
    ]
    for c in small:
        c.start()

    loads = [
        pltpu.make_async_copy(wg_ref.at[0], scr["wgu"].at[:, pl.ds(0, LANES)], load_sems.at[0]),
        pltpu.make_async_copy(wu_ref.at[0], scr["wgu"].at[:, pl.ds(LANES, LANES)], load_sems.at[1]),
        pltpu.make_async_copy(cache_ref.at[0, 0], scr["cache"], load_sems.at[2]),
    ]
    span = zl_n * width

    def down_block(i, which):
        off = pl.multiple_of((i * 2 + which) * span, LANES)
        return wd_ref.at[0, :, pl.ds(off, span)]

    loads += [
        pltpu.make_async_copy(
            down_block(i, core),
            scr["wd"].at[pl.ds(0, LANES), pl.ds(i * span, span)],
            load_sems.at[3 + i],
        )
        for i in range(nx)
    ]
    for c in loads:
        c.start()

    for c in small:
        c.wait()
    slot_ref, routes_ref, gate_ref, parent_ref, query_ref, kv_ref, hid_ref = held
    abuf, bbuf = scr["abuf"], scr["bbuf"]
    row = lax.broadcasted_iota(jnp.int32, (TOK, LANES), 0)
    lane = lax.broadcasted_iota(jnp.int32, (TOK, LANES), 1)
    weight = jnp.zeros((TOK, LANES), F32)
    for t in range(TOK):
        w = jnp.float32(0.0)
        for k in range(2):
            w += jnp.where(
                routes_ref[t // 4, k, t % 4] == expert, gate_ref[t // 4, k, t % 4], 0.0
            )
        weight = jnp.where(row == t, w, weight)
    high = weight.astype(BF).astype(F32)
    for h in range(HEADS):
        abuf[y, zh, pl.ds(h * TOK, TOK)] = (
            query_ref[:, h].astype(F32).reshape(TOK, LANES).astype(BF)
        )
    bbuf[zh, y, pl.ds(2 * TOK, TOK)] = jnp.where(
        lane == 0, high, jnp.where(lane == 1, weight - high, 0.0)
    ).astype(BF)
    for k in range(2):
        part = kv_ref[:, 0, k].astype(F32).reshape(TOK, LANES)
        bbuf[zh, y, pl.ds(k * TOK, TOK)] = part.astype(BF)

    pl.semaphore_wait(barrier, len(partners))

    other = scr["wd"].at[pl.ds(LANES, LANES)]
    wd_send, wd_recv = next(next_send), next(next_recv)
    for i in range(nx):
        transfer(
            down_block(i, 1 - core), other.at[:, pl.ds(i * span, span)], sibling, wd_send, wd_recv
        ).start()
    pending.append((other, wd_send))

    def gather_a():
        yield from gather(abuf.at[y], rzh)
        yield from gather(abuf, ry)

    def gather_b():
        yield from gather(bbuf.at[zh], ry)
        yield from gather(bbuf, rzh)

    interleave([gather_a(), gather_b()])

    def rows_a(k):
        return jnp.concatenate(
            [
                abuf[:, i, pl.ds(k * TOK, TOK)].astype(F32).reshape(ny * TOK, LANES)
                for i in range(zh_n)
            ],
            axis=0,
        )

    def rows_b(k):
        return bbuf[:, :, pl.ds(k * TOK, TOK)].astype(F32).reshape(tokens, LANES)

    new_k = rows_b(0).astype(BF)
    new_v = rows_b(1).astype(BF)
    loads[2].wait()
    old_k = scr["cache"][0]
    old_v = scr["cache"][1]
    contract = (((1,), (1,)), ((), ()))
    row_id = lax.broadcasted_iota(jnp.int32, (tokens, tokens), 0)
    col_id = lax.broadcasted_iota(jnp.int32, (tokens, tokens), 1)
    allowed = (row_id // 4 == col_id // 4) & (col_id <= row_id)
    scale = 1.0 / LANES**0.5
    node = jnp.int32(0)
    for k in range(leaves):
        node += jnp.where(slot_ref[k] == leaf, k, 0)
    children = leaves * 2
    token_child = lax.broadcasted_iota(jnp.int32, (tokens, children), 0) // 4
    child_id = lax.broadcasted_iota(jnp.int32, (tokens, children), 1)
    here_row = (token_child == child_id) & (parent_ref[...] == node)
    mine = jnp.sum(jnp.where(here_row, 1.0, 0.0), axis=1, keepdims=True)
    xp = [scr["xp0"], scr["xp1"], scr["xp2"]]
    own = scr["own"]
    start = scr["start"]
    xr = scr["xr"]
    mids = scr["xmid"]
    xs = scr["xs"]
    firsts = (ry, rz, ry)

    def home(p):
        first, second = (ry, rzh) if p < 2 else (rzh, ry)

        def keep(v):
            mids[p][...] = v.astype(BF)

        yield from scatter(xp[p], xr[p][0], first, keep)

        def final(v):
            w = v.astype(BF)
            xs[p] = w
            start[p][firsts[p].me] = w

        yield from scatter(mids[p], xr[p][1], second, final)
        yield from gather(start[p], firsts[p])

    homes = [home(p) for p in range(HEADS)]
    turns = (2, 0, 1)
    for p in turns:
        q = rows_a(p).astype(BF)
        s_old = lax.dot_general(q, old_k, contract, preferred_element_type=F32) * scale
        s_new = lax.dot_general(q, new_k, contract, preferred_element_type=F32) * scale
        s_new = jnp.where(allowed, s_new, -1e30)
        top = jnp.maximum(
            jnp.max(s_old, axis=1, keepdims=True), jnp.max(s_new, axis=1, keepdims=True)
        )
        e_old = jnp.exp(s_old - top)
        e_new = jnp.exp(s_new - top)
        total = jnp.sum(e_old, axis=1, keepdims=True) + jnp.sum(e_new, axis=1, keepdims=True)
        inv = 1.0 / total
        attn = jnp.dot((e_old * inv).astype(BF), old_v, preferred_element_type=F32)
        attn += jnp.dot((e_new * inv).astype(BF), new_v, preferred_element_type=F32)
        row = hid_ref[:, pl.ds(p * LANES, LANES)].astype(F32)
        here = jnp.where(mine > 0.5, attn + row, 0.0)
        here = here.reshape(zh_n, ny, TOK, LANES)
        if p < 2:
            for i in range(zh_n):
                xp[p][:, i] = here[i].astype(BF)
        else:
            xp[p][...] = here.astype(BF)
        next(homes[p])

    for _ in range(2):
        for p in turns:
            next(homes[p])

    sib = scr["sib"]
    d2d = []
    rings = {"x": rx, "y": ry, "z": rz}
    pieces = pieces_of(geom)

    def everywhere(k):
        p, low, many, two, three = pieces[k]
        two, three = rings[two], rings[three]
        own[k][three.me, two.me] = start[p][pl.ds(low, many)]
        yield from gather(own[k].at[three.me], two)

        send, recv = next(next_send), next(next_recv)

        def forward(index):
            transfer(own[k].at[index], sib[k].at[index], sibling, send, recv).start()

        pending.append((own[k], send))
        d2d.append((sib[k], recv))
        forward(three.me)
        yield from gather(own[k], three, forward)

    spread = [everywhere(k) for k in range(len(pieces))]
    for p in turns:
        interleave([homes[p]])
        for k in (0, 1, 2, 3, 4):
            if pieces[k][0] == p:
                next(spread[k])
    interleave([spread[k] for k in (0, 2, 4, 1, 3)])

    def tiles(refs, p, xi, m, i):
        zi = i * zl_n + m
        if p == 0:
            return [(refs[0].at[zi, xi], 0, cut_y), (refs[1].at[xi, zi], cut_y, ny - cut_y)]
        if p == 1:
            if i * zl_n < cut_z:
                return [(refs[2].at[:, xi, zi], 0, ny)]
            return [(refs[3].at[xi, :, zi - cut_z], 0, ny)]
        return [(refs[4].at[xi, zi], 0, ny)]

    def rows_of(refs, p, xi, m, i):
        parts = [ref[...].astype(F32) for ref, _, _ in tiles(refs, p, xi, m, i)]
        part = parts[0] if len(parts) == 1 else jnp.concatenate(parts, axis=0)
        return part.reshape(ny * TOK, LANES)

    acc = scr["acc"]
    acc[...] = jnp.zeros_like(acc)
    for c in loads[:2] + loads[3:]:
        c.wait()
    blocks = nx * zl_n

    def up(refs, which):
        @pl.loop(0, blocks)
        def _(j):
            xi, m = lax.div(j, zl_n), lax.rem(j, zl_n)
            cols = []
            for p in range(HEADS):
                cols.append(
                    jnp.concatenate(
                        [rows_of(refs, p, xi, m, i) for i in range(zh_n)],
                        axis=0,
                    ).astype(BF)
                )
            rows = jnp.concatenate(cols, axis=1)
            off = pl.multiple_of(((xi * 2 + which) * zl_n + m) * width, LANES)
            acc[...] += jnp.dot(rows, scr["wgu"][pl.ds(off, width), :], preferred_element_type=F32)

    up(own, core)
    for ref, recv in d2d:
        arrive(ref, recv)
    up(sib, 1 - core)

    gates = rows_b(2)
    gate = gates[:, 0:1] + gates[:, 1:2]
    g = acc[:, pl.ds(0, LANES)]
    u = acc[:, pl.ds(LANES, LANES)]
    units = (g * (1.0 / (1.0 + jnp.exp(-g))) * u).astype(BF).astype(F32)
    mine_units, other_units = scr["units"], scr["units_other"]
    mine_units[...] = (units * gate).astype(BF)
    u_send, u_recv = next(next_send), next(next_recv)
    transfer(mine_units, other_units, sibling, u_send, u_recv).start()
    pending.append((other_units, u_send))
    ho = scr["ho"]
    arrive(other, wd_recv)
    arrive(other_units, u_recv)

    def down(parts):
        count = len(parts) * LANES

        @pl.loop(0, blocks)
        def _(j):
            xi, m = lax.div(j, zl_n), lax.rem(j, zl_n)
            both = jnp.concatenate([mine_units[...], other_units[...]], axis=1)
            off = pl.multiple_of(j * width + parts[0] * LANES, LANES)
            o = jnp.dot(both, scr["wd"][:, pl.ds(off, count)], preferred_element_type=F32)
            for k, p in enumerate(parts):
                part = o[:, k * LANES : (k + 1) * LANES].reshape(zh_n, ny, TOK, LANES)
                for i in range(zh_n):
                    for ref, low, many in tiles(ho, p, xi, m, i):
                        ref[...] = part[i][low : low + many].astype(BF)

    gr, gmid, ends, er = scr["gr"], scr["gmid"], scr["ends"], scr["er"]

    def back(k):
        p, low, many, two, three = pieces[k]
        if k == 0:
            down((0, 1))
        if p == 2:
            down((2,))

        def keep(v):
            gmid[k][...] = v.astype(BF)

        def end(v):
            ends[p][pl.ds(low, many)] = v.astype(BF)

        yield from scatter(ho[k], gr[k][0], rings[three], keep)
        yield from scatter(gmid[k], gr[k][1], rings[two], end)

    def last(p):
        def final(v):
            w = (xs[p].astype(F32) + v).astype(BF)
            for c in range(2):
                out_ref[c, :, pl.ds(p * LANES, LANES)] = w[c * 4 : c * 4 + 4]

        yield from scatter(ends[p], er[p], firsts[p], final)

    backs = [back(k) for k in range(len(pieces))]
    lasts = [last(p) for p in range(HEADS)]
    for k in (4, 0, 2, 1, 3):
        next(backs[k])
    for k in (4, 1, 3, 0, 2):
        next(backs[k])
    for k in (4, 1, 3, 0, 2):
        interleave([backs[k]])
        if k in (4, 0, 2):
            next(lasts[pieces[k][0]])
    interleave([lasts[p] for p in (2, 0, 1)])

    for ref, send in pending:
        transfer(ref, ref, sibling, send, 0).wait_send()


def cuts_of(geom):
    nx, ny, zh_n, zl_n = geom
    return ny * 3 // 4, zh_n * 3 // 4 * zl_n


def pieces_of(geom):
    nx, ny, zh_n, zl_n = geom
    nz = zh_n * zl_n
    cut_y, cut_z = cuts_of(geom)
    return [
        (0, 0, cut_y, "x", "z"),
        (0, cut_y, ny - cut_y, "z", "x"),
        (1, 0, cut_z, "x", "y"),
        (1, cut_z, nz - cut_z, "y", "x"),
        (2, 0, ny, "z", "x"),
    ]


def scratch_of(geom, features, held):
    nx, ny, zh_n, zl_n = geom
    nz = zh_n * zl_n
    tokens = zh_n * ny * TOK
    tile = (TOK, LANES)
    vm = lambda *shape: pltpu.VMEM(shape + tile, BF)
    size = {"x": nx, "y": ny, "z": nz}
    pieces = pieces_of(geom)
    scr = {
        "send": pltpu.SemaphoreType.DMA((SENDS,)),
        "recv": pltpu.SemaphoreType.DMA((RECVS,)),
        "held": held,
        "small": pltpu.SemaphoreType.DMA((len(held),)),
        "load": pltpu.SemaphoreType.DMA((3 + nx,)),
        "cache": pltpu.VMEM((2, 256, LANES), BF),
        "wgu": pltpu.VMEM((features, 2 * LANES), BF),
        "wd": pltpu.VMEM((2 * LANES, features // 2), BF),
        "abuf": pltpu.VMEM((ny, zh_n, HEADS * TOK, LANES), BF),
        "bbuf": pltpu.VMEM((zh_n, ny, 3 * TOK, LANES), BF),
        "xs": vm(HEADS),
        "acc": pltpu.VMEM((tokens, 2 * LANES), F32),
        "units": pltpu.VMEM((tokens, LANES), BF),
        "units_other": pltpu.VMEM((tokens, LANES), BF),
    }
    for p in range(HEADS):
        scr["xp" + str(p)] = vm(ny, zh_n) if p < 2 else vm(zh_n, ny)
    for name in ("own", "sib", "ho"):
        scr[name] = [vm(size[three], size[two], many) for _, _, many, two, three in pieces]
    scr["start"] = [vm(n) for n in (ny, nz, ny)]
    scr["ends"] = [vm(n) for n in (ny, nz, ny)]
    scr["er"] = [vm(n - 1) for n in (ny, nz, ny)]
    scr["xmid"] = [vm(zh_n), vm(zh_n), vm(ny)]
    scr["xr"] = []
    for p in range(HEADS):
        first, second = (ny, zh_n) if p < 2 else (zh_n, ny)
        scr["xr"].append([vm(first - 1, second), vm(second - 1)])
    scr["gr"] = [
        [vm(size[three] - 1, size[two], many), vm(size[two] - 1, many)]
        for _, _, many, two, three in pieces
    ]
    scr["gmid"] = [vm(size[two], many) for _, _, many, two, three in pieces]
    return scr


def local(
    geom,
    node_cache,
    node_hidden,
    node_slot,
    parent,
    child_query,
    child_kv,
    routes,
    gate_w,
    w_gate,
    w_up,
    w_down,
):
    features = w_gate.shape[1]
    vmem = pl.BlockSpec(memory_space=pltpu.VMEM)
    hbm = pl.BlockSpec(memory_space=pl.ANY)
    operands = [
        node_slot,
        routes.transpose(0, 2, 1),
        gate_w.transpose(0, 2, 1),
        parent.reshape(1, -1),
        child_query.transpose(0, 2, 1, 3),
        child_kv,
        node_hidden,
    ]
    held = [pltpu.SMEM(v.shape, v.dtype) for v in operands[:3]]
    held += [pltpu.VMEM(v.shape, v.dtype) for v in operands[3:]]
    return pl.pallas_call(
        functools.partial(kernel, geom),
        out_shape=jax.ShapeDtypeStruct(child_query.shape[:2] + (HEADS * LANES,), BF),
        in_specs=[hbm] * (len(operands) + 4),
        out_specs=vmem,
        scratch_shapes=[scratch_of(geom, features, held)],
        compiler_params=pltpu.CompilerParams(
            collective_id=0, has_side_effects=True, vmem_limit_bytes=58 * 1024 * 1024
        ),
    )(
        *operands,
        node_cache,
        w_gate,
        w_up,
        w_down,
    )


def solution(mesh):
    leaves, experts, mp = mesh.shape["leaf"], mesh.shape["expert"], mesh.shape["mp"]
    geom = (experts // 2, NY, leaves // NY, mp)
    in_specs = (
        P("leaf", "expert", None, None, None),
        P("leaf", ("expert", "mp")),
        P(),
        P(),
        P("leaf", None, ("expert", "mp"), None),
        P("leaf", "expert", None, None, None),
        P("leaf", None, None),
        P("leaf", None, None),
        P("expert", None, ("leaf", "mp")),
        P("expert", None, ("leaf", "mp")),
        P("expert", ("leaf", "mp"), None),
    )
    out_specs = P("leaf", None, ("expert", "mp"))
    return jax.shard_map(
        functools.partial(local, geom),
        mesh=mesh,
        in_specs=in_specs,
        out_specs=out_specs,
        check_vma=False,
    )
```
